512 devices in a mesh: alpha: 16 (over y, x), beta: 32 (over z, core).
Axes of the slice: x: 4, y: 4, z: 16, core: 2. Of those that a mesh axis runs over, the one named last changes fastest.
Arguments:
- coeffs: bfloat16 [2048, 4096], P('alpha', 'beta'), may hold values from -6 to 6
- send_rows: int32 [256, 32], P('alpha'), may hold values from 0 to 127
- alpha_source: int32 [256, 2048], P(None, 'alpha'), may hold values from 0 to 511
- alpha_sign: int32 [256, 2048], P(None, 'alpha'), may hold values from -1 to 1, as said below
- beta_source: int32 [256, 4096], P('beta'), may hold values from 0 to 4095
- beta_sign: int32 [256, 4096], P('beta'), may hold values from -1 to 1, as said below
- integrals: bfloat16 [256, 256], replicated, may hold values from -0.0234375 to 0.0234375
Outputs:
- sigma: bfloat16 [2048, 4096], P('alpha', 'beta')
The draws below stay inside these ranges and needn't reach their ends.
Inputs may be any that keep to these rules, and one draw needn't show every extreme that they name: `alpha_sign`: each sign is -1 or 1. `beta_sign`: each sign is -1 or 1.
All inputs are finite; a program needn't handle non-finite values.
Results may differ from the reference program's by a relative error of at most 0.0049.
Values may be sent and summed in bfloat16 or wider, within the bound.
A program may use at most 64 MiB of HBM per device.

```python
import jax
import jax.numpy as jnp
from jax import lax

PAIRS = 256
ROWS_DEV = 128
CAP = 32
ALPHA_ROWS = 2048
BETA_COLS = 4096
N_ALPHA = 16


def draw_alpha_sign(key, part):
    key = jax.random.fold_in(key, 11)
    return (2 * jax.random.randint(key, (PAIRS, ALPHA_ROWS), 0, 2) - 1).astype(jnp.int32)


def draw_beta_sign(key, part):
    key = jax.random.fold_in(key, 23)
    return (2 * jax.random.randint(key, (PAIRS, BETA_COLS), 0, 2) - 1).astype(jnp.int32)


def touch_ends(array, stream_key, smallest, high):
    longest = array.shape.index(max(array.shape))
    spots = []
    for shift in (0, 1):
        where = [jax.random.randint(jax.random.fold_in(stream_key, axis), (), 0, length) for axis, length in enumerate(array.shape)]
        where[longest] = (where[longest] + shift) % array.shape[longest]
        spots.append(tuple(where))
    return array.at[spots[0]].set(smallest).at[spots[1]].set(high)


def steps_of(key, dims, cuts, low, top_value):
    gain, own = 1.0, jax.random.fold_in(key, 6)
    for axis_at, blocks in cuts:
        steps = jnp.exp(jax.random.uniform(jax.random.fold_in(own, axis_at), (blocks,), jnp.float32, low / len(cuts), top_value / len(cuts)))
        gain = gain * jnp.repeat(steps, dims[axis_at] // blocks).reshape([-1 if axis == axis_at else 1 for axis in range(len(dims))])
    return gain


def bell_draw(rng, dims, spread, reach, shards=(), kind=jnp.bfloat16):
    array = spread * jax.random.normal(rng, dims, jnp.float32)
    if shards:
        array = array * steps_of(rng, dims, shards, -0.22, 0.18)
    return jnp.clip(array, -reach, reach).astype(kind)


def setup_inputs(seed: int = 0) -> dict:
    seeds = jax.random.split(jax.random.key(seed), 8)
    coeffs = bell_draw(seeds[0], (ALPHA_ROWS, BETA_COLS), 1.0, 6.0, ((0, 16), (1, 32)))
    send_rows = touch_ends(jax.random.randint(seeds[1], (N_ALPHA * N_ALPHA, CAP), 0, ROWS_DEV), jax.random.fold_in(seeds[1], 1), 0, ROWS_DEV - 1).astype(jnp.int32)
    alpha_source = touch_ends(jax.random.randint(seeds[2], (PAIRS, ALPHA_ROWS), 0, N_ALPHA * CAP), jax.random.fold_in(seeds[2], 1), 0, (N_ALPHA * CAP) - 1).astype(jnp.int32)
    alpha_sign = draw_alpha_sign(jax.random.fold_in(seeds[7], 71), 0)
    beta_source = touch_ends(jax.random.randint(seeds[4], (PAIRS, BETA_COLS), 0, BETA_COLS), jax.random.fold_in(seeds[4], 1), 0, BETA_COLS - 1).astype(jnp.int32)
    beta_sign = draw_beta_sign(jax.random.fold_in(seeds[7], 71), 0)
    integrals = bell_draw(seeds[6], (PAIRS, PAIRS), (PAIRS * PAIRS) ** -0.5, 0.0234375)
    return {"coeffs": coeffs, "send_rows": send_rows, "alpha_source": alpha_source, "alpha_sign": alpha_sign, "beta_source": beta_source, "beta_sign": beta_sign, "integrals": integrals}


def reference(coeffs, send_rows, alpha_source, alpha_sign, beta_source, beta_sign, integrals):
    owner = (jnp.arange(ALPHA_ROWS) // ROWS_DEV).astype(jnp.int32)
    sender = (alpha_source // CAP).astype(jnp.int32)
    slot_index = (alpha_source % CAP).astype(jnp.int32)
    routed = send_rows.reshape(N_ALPHA, N_ALPHA, CAP)
    partner_index = (sender * ROWS_DEV + routed[sender, owner[None, :], slot_index]).astype(jnp.int32)
    weights = integrals.astype(jnp.float32)
    blocks = ALPHA_ROWS // 32
    source_blocks = partner_index.reshape(PAIRS, blocks, 32).transpose(1, 0, 2)
    sign_blocks = alpha_sign.reshape(PAIRS, blocks, 32).transpose(1, 0, 2)
    beta_weights = beta_sign.astype(jnp.float32)

    def one_block(pieces):
        rows_index, signs = pieces
        excited = coeffs[rows_index] * signs[:, :, None].astype(jnp.bfloat16)
        mixed = jnp.einsum("pq,qrc->prc", weights, excited.astype(jnp.float32)).astype(jnp.bfloat16)
        moved = jnp.take_along_axis(mixed, beta_source[:, None, :], axis=2)
        return jnp.einsum("prc,pc->rc", moved.astype(jnp.float32), beta_weights).astype(jnp.bfloat16)

    result = lax.map(one_block, (source_blocks, sign_blocks))
    return result.reshape(ALPHA_ROWS, BETA_COLS)
```

```python
import functools

import jax
import jax.numpy as jnp
from jax import lax
from jax.experimental import pallas as pl
from jax.experimental.pallas import tpu as pltpu
from jax.sharding import PartitionSpec as P

MESH = pl.DeviceIdType.MESH
BF16, F32, I32 = jnp.bfloat16, jnp.float32, jnp.int32
BLK = 128
NP = 8
HALF = 64
UNIT = 4
LEAD = 8


def kernel(
    n_alpha, n_z,
    coeffs, send_rows, a_source, a_sign, b_source, b_sign, integrals,
    out,
    picked, received, table, src_t, sgn_t, v16, w_raw, w_out, w_full, w_t, big, idx_v, idx_s,
    rs_in, rs_out, sib_in, sib_out,
    pick_send, pick_recv, ring_send, ring_recv, half_send, half_recv, w_send, w_recv,
    rs_send, rs_recv, sib_send, sib_recv, idx_sem,
):
    a = lax.axis_index("alpha")
    b = lax.axis_index("beta")
    z, core = b // 2, b % 2
    cap = send_rows.shape[1]
    slots = n_alpha * cap
    n_pairs = integrals.shape[0]
    cols = b_source.shape[1]
    steps = n_z // 2
    first = 4 if steps >= 4 else 2
    units = HALF // UNIT
    units_pre = units - 4 * (first - 2)

    up = lax.rem(z + 1, n_z) * 2 + core
    down = lax.rem(z + n_z - 1, n_z) * 2 + core
    other = z * 2 + 1 - core

    barrier = pltpu.get_barrier_semaphore()
    for o in range(1, n_alpha):
        pl.semaphore_signal(barrier, inc=1, device_id=(lax.rem(a + o, n_alpha), b), device_id_type=MESH)
    for peer in (up, down, other):
        pl.semaphore_signal(barrier, inc=1, device_id=(a, peer), device_id_type=MESH)

    per = BLK // cap
    row_ids = lax.broadcasted_iota(I32, (BLK, BLK), 0)
    local = coeffs[...]
    for g in range(slots // BLK):
        line = jnp.concatenate([send_rows[g * per + k : g * per + k + 1, :] for k in range(per)], axis=1)
        hot = jnp.where(row_ids == line, 1.0, 0.0).T.astype(BF16)
        picked[g * BLK : (g + 1) * BLK, :] = jnp.dot(hot, local, preferred_element_type=F32).astype(BF16)
    pl.semaphore_wait(barrier, n_alpha - 1 + 3)

    def pick_copy(to, frm):
        return pltpu.make_async_remote_copy(
            src_ref=picked.at[pl.ds(pl.multiple_of(to * cap, cap), cap), :],
            dst_ref=received.at[pl.ds(pl.multiple_of(frm * cap, cap), cap), :],
            send_sem=pick_send.at[to], recv_sem=pick_recv.at[frm],
            device_id=(to, b), device_id_type=MESH)

    @pl.loop(1, n_alpha)
    def _(o):
        pick_copy(lax.rem(a + o, n_alpha), a).start()

    mine = pl.ds(pl.multiple_of(a * cap, cap), cap)
    received[mine, :] = picked[mine, :]

    src_t[...] = a_source[...].astype(F32).T
    sgn_t[...] = a_sign[...].astype(F32).T
    r16 = lax.broadcasted_iota(I32, (2 * NP, n_pairs), 0)
    c16 = lax.broadcasted_iota(I32, (2 * NP, n_pairs), 1)
    want = jnp.where(r16 < NP, b * NP + r16, other * NP + r16 - NP)
    v16[...] = jnp.dot(
        jnp.where(c16 == want, 1.0, 0.0).astype(BF16), integrals[...], preferred_element_type=F32).astype(BF16)
    pair_at = lax.broadcasted_iota(I32, (NP, BLK), 0) * (2 * cols) + LEAD
    pair_at = pair_at - lax.rem(lax.broadcasted_iota(I32, (NP, BLK), 1), 8)
    for c in range(cols // BLK):
        cut = slice(c * BLK, (c + 1) * BLK)
        idx_v[c] = b_source[:, cut] + jnp.where(b_sign[:, cut] < 0, cols, 0) + pair_at

    slot_ids = lax.broadcasted_iota(I32, (slots, n_pairs), 0).astype(F32)

    def weight_unit(unit):
        for k in range(UNIT):
            at = unit * UNIT + k
            line = pl.ds(core * HALF + at, 1)
            hot = jnp.where(slot_ids == src_t[line, :], sgn_t[line, :], 0.0).astype(BF16)
            w_raw[at] = lax.dot_general(v16[...], hot, (((1,), (1,)), ((), ())), preferred_element_type=F32)

    @pl.loop(0, units_pre)
    def _(unit):
        weight_unit(unit)

    @pl.loop(1, n_alpha)
    def _(o):
        pick_copy(a, lax.rem(a + o, n_alpha)).wait_recv()

    table[b] = received[...].astype(F32).T.astype(BF16)

    def half_rows(h):
        return pl.ds(pl.multiple_of(h * HALF, HALF), HALF)

    def ring_copy(m, origin, d, h):
        ref = table.at[origin * 2 + core, half_rows(h), :]
        return pltpu.make_async_remote_copy(
            src_ref=ref, dst_ref=ref, send_sem=ring_send.at[m], recv_sem=ring_recv.at[m],
            device_id=(a, jnp.where(d == 0, up, down)), device_id_type=MESH)

    def half_copy(n, h, origin, who):
        ref = table.at[origin * 2 + who, half_rows(h), :]
        return pltpu.make_async_remote_copy(
            src_ref=ref, dst_ref=ref, send_sem=half_send.at[n * 2 + h], recv_sem=half_recv.at[n * 2 + h],
            device_id=(a, other), device_id_type=MESH)

    for h in range(2):
        for d in range(2):
            ring_copy(h * 2 + d, z, d, h).start()
    for h in range(2):
        half_copy(0, h, z, core).start()

    def w_copy():
        return pltpu.make_async_remote_copy(
            src_ref=w_out, dst_ref=w_full.at[:, half_rows(core), :],
            send_sem=w_send, recv_sem=w_recv, device_id=(a, other), device_id_type=MESH)

    def w_wait():
        return pltpu.make_async_remote_copy(
            src_ref=w_out, dst_ref=w_full.at[:, half_rows(1 - core), :],
            send_sem=w_send, recv_sem=w_recv, device_id=(a, other), device_id_type=MESH)

    def origin_of(n):
        s = (n + 1) // 2
        return lax.rem(jnp.where(n % 2 == 1, z - s, z + s) + n_z, n_z)

    def mix(n):
        origin = origin_of(n)
        for h in range(2):
            half_copy(n, h, origin, 1 - core).wait_recv()
        rows = table[pl.ds(origin * 2, 2)].reshape(2 * BLK, slots)
        for p in range(0, NP, 2):
            r = jnp.dot(rows, w_t[:, p * BLK : (p + 2) * BLK], preferred_element_type=F32)
            for k in range(2):
                at = LEAD + (p + k) * 2 * cols + origin * (2 * BLK)
                x = r[:, k * BLK : (k + 1) * BLK]
                big[pl.ds(pl.multiple_of(at, 8), 2 * BLK), :] = x
                big[pl.ds(pl.multiple_of(at + cols, 8), 2 * BLK), :] = -x

    def target(s):
        return jnp.maximum(jnp.minimum(4 * (s - first) + 3, 2 * s - 1), 0)

    @pl.loop(0, 4 * steps)
    def _(m):
        s, d, h = m // 4 + 1, m % 2, (m % 4) // 2
        origin = lax.rem(jnp.where(d == 0, z - s, z + s) + n_z, n_z)
        exists = jnp.logical_or(s < steps, d == h)
        onward = jnp.logical_or(s + 1 < steps, jnp.logical_and(s + 1 == steps, d == h))

        @pl.when(exists)
        def _():
            ring_copy(m, origin, d, h).wait_recv()

        @pl.when(onward)
        def _():
            ring_copy(m + 4, origin, d, h).start()

        @pl.when(exists)
        def _():
            half_copy(jnp.minimum(2 * s - 1 + d, n_z - 1), h, origin, core).start()

        if first > 2:
            @pl.when(m < 4 * (first - 2))
            def _():
                weight_unit(units_pre + m)

        @pl.when(m == 4 * (first - 2))
        def _():
            for p in range(NP):
                w_out[p] = w_raw[:, NP + p, :].astype(BF16)
            w_copy().start()
            for p in range(NP):
                w_full[p, half_rows(core), :] = w_raw[:, p, :].astype(BF16)

        @pl.when(m == 4 * (first - 1) - 1)
        def _():
            w_wait().wait_recv()
            for p in range(NP):
                w_t[:, p * BLK : (p + 1) * BLK] = w_full[p].astype(F32).T.astype(BF16)

        low, high = target(s - 1), target(s)
        k = m % 4

        @pl.loop(low + ((high - low) * k) // 4, low + ((high - low) * (k + 1)) // 4)
        def _(n):
            mix(n)

    def owner_of(i):
        t = i // 2
        away = jnp.where(i == n_z - 1, 0, jnp.where(i % 2 == 0, steps - t, t + 1 - steps))
        return lax.rem(z + away + n_z, n_z)

    def idx_copy(i, which):
        chunk = owner_of(i) * 2 + jnp.where(which == 0, 1 - core, core)
        return pltpu.make_async_copy(idx_v.at[chunk], idx_s.at[which], idx_sem.at[which])

    for which in range(2):
        idx_copy(0, which).start()

    @pl.loop(target(steps), n_z)
    def _(n):
        mix(n)

    sub = lax.broadcasted_iota(I32, (8, BLK), 0)

    def gather(which, dst):
        for u in range(BLK // 8):
            total = None
            for k in range(8):
                acc = None
                for p in range(NP):
                    v = big[pl.ds(idx_s[which, p, u * 8 + k], 8), :]
                    acc = v if acc is None else acc + v
                total = acc if total is None else jnp.where(sub == k, acc, total)
            dst[u * 8 : (u + 1) * 8, :] = total

    def sib_copy(i):
        return pltpu.make_async_remote_copy(
            src_ref=sib_out.at[i], dst_ref=sib_in.at[i], send_sem=sib_send.at[i], recv_sem=sib_recv.at[i],
            device_id=(a, other), device_id_type=MESH)

    def rs_copy(i):
        return pltpu.make_async_remote_copy(
            src_ref=rs_out.at[i], dst_ref=rs_in.at[i], send_sem=rs_send.at[i], recv_sem=rs_recv.at[i],
            device_id=(a, jnp.where(i % 2 == 0, up, down)), device_id_type=MESH)

    def pass_on(i):
        sib_copy(i).wait_recv()
        rs_out[i] = rs_out[i] + sib_in[i]

        @pl.when(i >= 2)
        def _():
            rs_copy(i - 2).wait_recv()
            rs_out[i] = rs_out[i] + rs_in[i - 2]

        rs_copy(i).start()

    @pl.loop(0, n_z)
    def _(i):
        idx_copy(i, 0).wait()
        gather(0, sib_out.at[i])
        sib_copy(i).start()

        @pl.when(i + 1 < n_z)
        def _():
            idx_copy(i + 1, 0).start()

        @pl.when(i > 0)
        def _():
            pass_on(i - 1)

        idx_copy(i, 1).wait()
        gather(1, rs_out.at[i])

        @pl.when(i + 1 < n_z)
        def _():
            idx_copy(i + 1, 1).start()

    last = n_z - 1
    sib_copy(last).wait_recv()
    rs_copy(last - 2).wait_recv()
    rs_copy(last - 1).wait_recv()
    total = (rs_out[last] + sib_in[last]) + (rs_in[last - 2] + rs_in[last - 1])
    out[...] = total.T.astype(BF16)

    @pl.loop(1, n_alpha)
    def _(o):
        pick_copy(lax.rem(a + o, n_alpha), a).wait_send()

    @pl.loop(0, 4 * steps)
    def _(m):
        s, d, h = m // 4 + 1, m % 2, (m % 4) // 2

        @pl.when(jnp.logical_or(s < steps, d == h))
        def _():
            ring_copy(m, z, d, h).wait_send()

    @pl.loop(0, 2 * n_z)
    def _(j):
        half_copy(j // 2, j % 2, z, core).wait_send()

    w_copy().wait_send()

    @pl.loop(0, n_z)
    def _(i):
        sib_copy(i).wait_send()

        @pl.when(i < n_z - 1)
        def _():
            rs_copy(i).wait_send()


def body(n_alpha, n_z, coeffs, send_rows, a_source, a_sign, b_source, b_sign, integrals):
    cap = send_rows.shape[1]
    slots = n_alpha * cap
    n_pairs = integrals.shape[0]
    cols = b_source.shape[1]
    V, DMA = pltpu.VMEM, pltpu.SemaphoreType.DMA
    blocks = 2 * n_z
    scratch = [
        V((slots, BLK), BF16), V((slots, BLK), BF16), V((blocks, BLK, slots), BF16),
        V((BLK, n_pairs), F32), V((BLK, n_pairs), F32), V((2 * NP, n_pairs), BF16),
        V((HALF, 2 * NP, slots), F32), V((NP, HALF, slots), BF16), V((NP, BLK, slots), BF16),
        V((slots, NP * BLK), BF16), V((NP * 2 * cols + 2 * LEAD, BLK), F32),
        V((cols // BLK, NP, BLK), I32), pltpu.SMEM((2, NP, BLK), I32),
        V((n_z, BLK, BLK), F32), V((n_z, BLK, BLK), F32), V((n_z, BLK, BLK), F32), V((n_z, BLK, BLK), F32),
        DMA((n_alpha,)), DMA((n_alpha,)), DMA((2 * n_z,)), DMA((2 * n_z,)), DMA((2 * n_z,)), DMA((2 * n_z,)),
        DMA, DMA, DMA((n_z,)), DMA((n_z,)), DMA((n_z,)), DMA((n_z,)), DMA((2,)),
    ]
    return pl.pallas_call(
        functools.partial(kernel, n_alpha, n_z),
        out_shape=jax.ShapeDtypeStruct((BLK, BLK), BF16),
        in_specs=[pl.BlockSpec(memory_space=V)] * 7,
        out_specs=pl.BlockSpec(memory_space=V),
        scratch_shapes=scratch,
        compiler_params=pltpu.CompilerParams(
            collective_id=0, has_side_effects=True, vmem_limit_bytes=60 * 2**20),
    )(coeffs, send_rows, a_source, a_sign, b_source, b_sign, integrals)


def solution(mesh):
    in_specs = (
        P("alpha", "beta"), P("alpha", None), P(None, "alpha"), P(None, "alpha"),
        P("beta", None), P("beta", None), P(),
    )
    run = functools.partial(body, mesh.shape["alpha"], mesh.shape["beta"] // 2)
    return jax.shard_map(run, mesh=mesh, in_specs=in_specs, out_specs=P("alpha", "beta"), check_vma=False)
```

```python
import functools

import jax
import jax.numpy as jnp
from jax import lax
from jax.experimental import pallas as pl
from jax.experimental.pallas import tpu as pltpu
from jax.sharding import PartitionSpec as P

MESH = pl.DeviceIdType.MESH
BF16, F32, I32 = jnp.bfloat16, jnp.float32, jnp.int32
BLK = 128
NP = 8
HALF = 64
PARTS = 4
PART = BLK // PARTS
ROUND = 2 * PARTS
UNIT = 4
LEAD = 8
LAG = 5


def kernel(
    n_alpha, n_z,
    coeffs, send_rows, a_source, a_sign, b_source, b_sign, integrals,
    out,
    picked, received, table, src_t, sgn_t, v16, w_raw, w_out, w_full, w_t, big, idx_v, idx_s,
    rs_in, rs_out, mate_in, mate_out, terms, sib_in, sib_out,
    pick_send, pick_recv, ring_send, ring_recv, half_send, half_recv, w_send, w_recv,
    rs_send, rs_recv, mate_send, mate_recv, sib_send, sib_recv, idx_sem,
):
    a = lax.axis_index("alpha")
    b = lax.axis_index("beta")
    z, core = b // 2, b % 2
    cap = send_rows.shape[1]
    slots = n_alpha * cap
    n_pairs = integrals.shape[0]
    cols = b_source.shape[1]
    steps = n_z // 2
    first = 4 if steps >= 4 else 2
    units = HALF // UNIT
    units_pre = units - ROUND // 2 * (first - 2)

    up = lax.rem(z + 1, n_z) * 2 + core
    down = lax.rem(z + n_z - 1, n_z) * 2 + core
    other = z * 2 + 1 - core

    barrier = pltpu.get_barrier_semaphore()
    for o in range(1, n_alpha):
        pl.semaphore_signal(barrier, inc=1, device_id=(lax.rem(a + o, n_alpha), b), device_id_type=MESH)
    for peer in (up, down, other):
        pl.semaphore_signal(barrier, inc=1, device_id=(a, peer), device_id_type=MESH)

    per = BLK // cap
    row_ids = lax.broadcasted_iota(I32, (BLK, BLK), 0)
    local = coeffs[...]
    for g in range(slots // BLK):
        line = jnp.concatenate([send_rows[g * per + k : g * per + k + 1, :] for k in range(per)], axis=1)
        hot = jnp.where(row_ids == line, 1.0, 0.0).T.astype(BF16)
        picked[g * BLK : (g + 1) * BLK, :] = jnp.dot(hot, local, preferred_element_type=F32).astype(BF16)
    pl.semaphore_wait(barrier, n_alpha - 1 + 3)

    def pick_copy(to, frm):
        return pltpu.make_async_remote_copy(
            src_ref=picked.at[pl.ds(pl.multiple_of(to * cap, cap), cap), :],
            dst_ref=received.at[pl.ds(pl.multiple_of(frm * cap, cap), cap), :],
            send_sem=pick_send.at[to], recv_sem=pick_recv.at[frm],
            device_id=(to, b), device_id_type=MESH)

    @pl.loop(1, n_alpha)
    def _(o):
        pick_copy(lax.rem(a + o, n_alpha), a).start()

    mine = pl.ds(pl.multiple_of(a * cap, cap), cap)
    received[mine, :] = picked[mine, :]

    src_t[...] = a_source[...].astype(F32).T
    sgn_t[...] = a_sign[...].astype(F32).T
    r16 = lax.broadcasted_iota(I32, (2 * NP, n_pairs), 0)
    c16 = lax.broadcasted_iota(I32, (2 * NP, n_pairs), 1)
    want = jnp.where(r16 < NP, b * NP + r16, other * NP + r16 - NP)
    v16[...] = jnp.dot(
        jnp.where(c16 == want, 1.0, 0.0).astype(BF16), integrals[...], preferred_element_type=F32).astype(BF16)
    pair_at = lax.broadcasted_iota(I32, (NP, BLK), 0) * (2 * cols) + LEAD
    pair_at = pair_at - lax.rem(lax.broadcasted_iota(I32, (NP, BLK), 1), 8)
    for c in range(cols // BLK):
        cut = slice(c * BLK, (c + 1) * BLK)
        idx_v[c] = b_source[:, cut] + jnp.where(b_sign[:, cut] < 0, cols, 0) + pair_at

    slot_ids = lax.broadcasted_iota(I32, (slots, n_pairs), 0).astype(F32)

    def weight_unit(unit):
        for k in range(UNIT):
            at = unit * UNIT + k
            line = pl.ds(core * HALF + at, 1)
            hot = jnp.where(slot_ids == src_t[line, :], sgn_t[line, :], 0.0).astype(BF16)
            w_raw[at] = lax.dot_general(v16[...], hot, (((1,), (1,)), ((), ())), preferred_element_type=F32)

    @pl.loop(0, units_pre)
    def _(unit):
        weight_unit(unit)

    @pl.loop(1, n_alpha)
    def _(o):
        pick_copy(a, lax.rem(a + o, n_alpha)).wait_recv()

    table[b] = received[...].astype(F32).T.astype(BF16)

    def half_rows(h):
        return pl.ds(pl.multiple_of(h * HALF, HALF), HALF)

    def ring_copy(m, origin, d, h):
        ref = table.at[origin * 2 + core, pl.ds(pl.multiple_of(h * PART, PART), PART), :]
        return pltpu.make_async_remote_copy(
            src_ref=ref, dst_ref=ref, send_sem=ring_send.at[m], recv_sem=ring_recv.at[m],
            device_id=(a, jnp.where(d == 0, up, down)), device_id_type=MESH)

    def half_copy(n, h, origin, who):
        ref = table.at[origin * 2 + who, half_rows(h), :]
        return pltpu.make_async_remote_copy(
            src_ref=ref, dst_ref=ref, send_sem=half_send.at[n * 2 + h], recv_sem=half_recv.at[n * 2 + h],
            device_id=(a, other), device_id_type=MESH)

    for h in range(PARTS):
        for d in range(2):
            ring_copy(h * 2 + d, z, d, h).start()
    for h in range(2):
        half_copy(0, h, z, core).start()

    def w_copy():
        return pltpu.make_async_remote_copy(
            src_ref=w_out, dst_ref=w_full.at[:, half_rows(core), :],
            send_sem=w_send, recv_sem=w_recv, device_id=(a, other), device_id_type=MESH)

    def w_wait():
        return pltpu.make_async_remote_copy(
            src_ref=w_out, dst_ref=w_full.at[:, half_rows(1 - core), :],
            send_sem=w_send, recv_sem=w_recv, device_id=(a, other), device_id_type=MESH)

    def origin_of(n):
        s = (n + 1) // 2
        return lax.rem(jnp.where(n % 2 == 1, z - s, z + s) + n_z, n_z)

    def mix(n):
        origin = origin_of(n)
        for h in range(2):
            half_copy(n, h, origin, 1 - core).wait_recv()
        rows = table[pl.ds(origin * 2, 2)].reshape(2 * BLK, slots)
        for p in range(0, NP, 2):
            r = jnp.dot(rows, w_t[:, p * BLK : (p + 2) * BLK], preferred_element_type=F32)
            for k in range(2):
                at = LEAD + (p + k) * 2 * cols + origin * (2 * BLK)
                x = r[:, k * BLK : (k + 1) * BLK]
                big[pl.ds(pl.multiple_of(at, 8), 2 * BLK), :] = x
                big[pl.ds(pl.multiple_of(at + cols, 8), 2 * BLK), :] = -x

    def target(s):
        return jnp.maximum(jnp.minimum(4 * (s - first) + 3, 2 * s - 1), 0)

    @pl.loop(0, ROUND * steps)
    def _(m):
        s, d, h = m // ROUND + 1, m % 2, (m % ROUND) // 2
        origin = lax.rem(jnp.where(d == 0, z - s, z + s) + n_z, n_z)
        its_way = d == h // (PARTS // 2)
        exists = jnp.logical_or(s < steps, its_way)
        onward = jnp.logical_or(s + 1 < steps, jnp.logical_and(s + 1 == steps, its_way))

        @pl.when(exists)
        def _():
            ring_copy(m, origin, d, h).wait_recv()

        @pl.when(onward)
        def _():
            ring_copy(m + ROUND, origin, d, h).start()

        @pl.when(jnp.logical_and(exists, h % 2 == 1))
        def _():
            half_copy(jnp.minimum(2 * s - 1 + d, n_z - 1), h // 2, origin, core).start()

        if first > 2:
            @pl.when(jnp.logical_and(m < ROUND * (first - 2), m % 2 == 0))
            def _():
                weight_unit(units_pre + m // 2)

        @pl.when(m == ROUND * (first - 2))
        def _():
            for p in range(NP):
                w_out[p] = w_raw[:, NP + p, :].astype(BF16)
            w_copy().start()
            for p in range(NP):
                w_full[p, half_rows(core), :] = w_raw[:, p, :].astype(BF16)

        @pl.when(m == ROUND * (first - 1) - 1)
        def _():
            w_wait().wait_recv()
            for p in range(NP):
                w_t[:, p * BLK : (p + 1) * BLK] = w_full[p].astype(F32).T.astype(BF16)

        low, high = target(s - 1), target(s)
        k = m % ROUND

        @pl.loop(low + ((high - low) * k) // ROUND, low + ((high - low) * (k + 1)) // ROUND)
        def _(n):
            mix(n)

    side = jnp.where(z % 2 == 1, 1, -1)
    mate = lax.rem(z - side + n_z, n_z)

    def owner_of(i):
        far = steps - 1 - i // 2
        return lax.rem(jnp.where(i % 2 == 1, z + side * far, mate - side * far) + n_z, n_z)

    def idx_copy(i, which):
        chunk = owner_of(i) * 2 + jnp.where(which == 0, 1 - core, core)
        return pltpu.make_async_copy(idx_v.at[chunk], idx_s.at[which], idx_sem.at[which])

    for which in range(2):
        idx_copy(0, which).start()

    @pl.loop(target(steps), n_z)
    def _(n):
        mix(n)

    sub = lax.broadcasted_iota(I32, (8, BLK), 0)

    def gather(which, dst):
        for u in range(BLK // 8):
            total = None
            for k in range(8):
                acc = None
                for p in range(NP):
                    v = big[pl.ds(idx_s[which, p, u * 8 + k], 8), :]
                    acc = v if acc is None else acc + v
                total = acc if total is None else jnp.where(sub == k, acc, total)
            dst[u * 8 : (u + 1) * 8, :] = total

    def sib_copy(i):
        return pltpu.make_async_remote_copy(
            src_ref=sib_out.at[i], dst_ref=sib_in.at[i], send_sem=sib_send.at[i], recv_sem=sib_recv.at[i],
            device_id=(a, other), device_id_type=MESH)

    def mate_copy(t):
        return pltpu.make_async_remote_copy(
            src_ref=mate_out.at[t], dst_ref=mate_in.at[t], send_sem=mate_send.at[t], recv_sem=mate_recv.at[t],
            device_id=(a, mate * 2 + core), device_id_type=MESH)

    def rs_copy(t):
        return pltpu.make_async_remote_copy(
            src_ref=rs_out.at[t], dst_ref=rs_in.at[t], send_sem=rs_send.at[t], recv_sem=rs_recv.at[t],
            device_id=(a, owner_of(2 * t + 1) * 2 + core), device_id_type=MESH)

    def pass_on(t):
        mate_copy(t).wait_recv()
        rs_out[t] = (terms[2 * t + 1] + mate_in[t].astype(F32)).astype(BF16)
        rs_copy(t).start()

    def chip_sum(i):
        sib_copy(i).wait_recv()
        terms[i] = terms[i] + sib_in[i]

        @pl.when(i % 2 == 0)
        def _():
            mate_out[i // 2] = terms[i].astype(BF16)
            mate_copy(i // 2).start()

    @pl.loop(0, n_z)
    def _(i):
        idx_copy(i, 0).wait()
        gather(0, sib_out.at[i])
        sib_copy(i).start()

        @pl.when(i + 1 < n_z)
        def _():
            idx_copy(i + 1, 0).start()

        @pl.when(i > 0)
        def _():
            chip_sum(i - 1)

        @pl.when(jnp.logical_and(i % 2 == 1, i >= LAG))
        def _():
            pass_on((i - LAG) // 2)

        idx_copy(i, 1).wait()
        gather(1, terms.at[i])

        @pl.when(i + 1 < n_z)
        def _():
            idx_copy(i + 1, 1).start()

    last = n_z - 1
    for t in range((last - LAG) // 2 + 1, steps - 1):
        pass_on(t)
    chip_sum(last)
    mate_copy(steps - 1).wait_recv()
    total = terms[last] + mate_in[steps - 1].astype(F32)
    for t in range(steps - 1):
        rs_copy(t).wait_recv()
        total = total + rs_in[t].astype(F32)
    out[...] = total.T.astype(BF16)

    @pl.loop(1, n_alpha)
    def _(o):
        pick_copy(lax.rem(a + o, n_alpha), a).wait_send()

    @pl.loop(0, ROUND * steps)
    def _(m):
        s, d, h = m // ROUND + 1, m % 2, (m % ROUND) // 2

        @pl.when(jnp.logical_or(s < steps, d == h // (PARTS // 2)))
        def _():
            ring_copy(m, z, d, h).wait_send()

    @pl.loop(0, 2 * n_z)
    def _(j):
        half_copy(j // 2, j % 2, z, core).wait_send()

    w_copy().wait_send()

    @pl.loop(0, n_z)
    def _(i):
        sib_copy(i).wait_send()

    @pl.loop(0, steps)
    def _(t):
        mate_copy(t).wait_send()

        @pl.when(t < steps - 1)
        def _():
            rs_copy(t).wait_send()


def body(n_alpha, n_z, coeffs, send_rows, a_source, a_sign, b_source, b_sign, integrals):
    cap = send_rows.shape[1]
    slots = n_alpha * cap
    n_pairs = integrals.shape[0]
    cols = b_source.shape[1]
    V, DMA = pltpu.VMEM, pltpu.SemaphoreType.DMA
    blocks, half = 2 * n_z, n_z // 2
    scratch = [
        V((slots, BLK), BF16), V((slots, BLK), BF16), V((blocks, BLK, slots), BF16),
        V((BLK, n_pairs), F32), V((BLK, n_pairs), F32), V((2 * NP, n_pairs), BF16),
        V((HALF, 2 * NP, slots), F32), V((NP, HALF, slots), BF16), V((NP, BLK, slots), BF16),
        V((slots, NP * BLK), BF16), V((NP * 2 * cols + 2 * LEAD, BLK), F32),
        V((cols // BLK, NP, BLK), I32), pltpu.SMEM((2, NP, BLK), I32),
        V((half, BLK, BLK), BF16), V((half, BLK, BLK), BF16), V((half, BLK, BLK), BF16), V((half, BLK, BLK), BF16),
        V((n_z, BLK, BLK), F32), V((n_z, BLK, BLK), F32), V((n_z, BLK, BLK), F32),
        DMA((n_alpha,)), DMA((n_alpha,)), DMA((PARTS * n_z,)), DMA((PARTS * n_z,)),
        DMA((2 * n_z,)), DMA((2 * n_z,)),
        DMA, DMA, DMA((half,)), DMA((half,)), DMA((half,)), DMA((half,)), DMA((n_z,)), DMA((n_z,)), DMA((2,)),
    ]
    return pl.pallas_call(
        functools.partial(kernel, n_alpha, n_z),
        out_shape=jax.ShapeDtypeStruct((BLK, BLK), BF16),
        in_specs=[pl.BlockSpec(memory_space=V)] * 7,
        out_specs=pl.BlockSpec(memory_space=V),
        scratch_shapes=scratch,
        compiler_params=pltpu.CompilerParams(
            collective_id=0, has_side_effects=True, vmem_limit_bytes=60 * 2**20),
    )(coeffs, send_rows, a_source, a_sign, b_source, b_sign, integrals)


def solution(mesh):
    in_specs = (
        P("alpha", "beta"), P("alpha", None), P(None, "alpha"), P(None, "alpha"),
        P("beta", None), P("beta", None), P(),
    )
    run = functools.partial(body, mesh.shape["alpha"], mesh.shape["beta"] // 2)
    return jax.shard_map(run, mesh=mesh, in_specs=in_specs, out_specs=P("alpha", "beta"), check_vma=False)
```

```python
import functools

import jax
import jax.numpy as jnp
from jax import lax
from jax.experimental import pallas as pl
from jax.experimental.pallas import tpu as pltpu
from jax.sharding import PartitionSpec as P

MESH = pl.DeviceIdType.MESH
BF16, F32, I32 = jnp.bfloat16, jnp.float32, jnp.int32
BLK = 128
NP = 8
HALF = 64
PARTS = 4
PART = BLK // PARTS
ROUND = 2 * PARTS
UNIT = 4
LEAD = 8
LAG = 5
HOPS = 5
FAR = 6
GROUPS = ((0, 2), (2, 3))


def kernel(
    n_alpha, n_z,
    coeffs, send_rows, a_source, a_sign, b_source, b_sign, integrals,
    out,
    picked, received, hot, raw, far_picked, far_received, table, src_t, sgn_t, v16, w_raw, w_out, w_full, w_t, big, idx_v, idx_s,
    rs_in, rs_out, mate_in, mate_out, terms, sib_in, sib_out,
    pick_send, pick_recv, raw_send, raw_recv, far_send, far_recv, ring_send, ring_recv, half_send, half_recv, w_send, w_recv,
    rs_send, rs_recv, mate_send, mate_recv, sib_send, sib_recv, idx_sem,
):
    a = lax.axis_index("alpha")
    b = lax.axis_index("beta")
    z, core = b // 2, b % 2
    cap = send_rows.shape[1]
    slots = n_alpha * cap
    n_pairs = integrals.shape[0]
    cols = b_source.shape[1]
    steps = n_z // 2
    units = HALF // UNIT

    def along(away):
        return lax.rem(z + away + n_z, n_z) * 2 + core

    up, down = along(1), along(-1)
    other = z * 2 + 1 - core

    barrier = pltpu.get_barrier_semaphore()
    for o in range(1, n_alpha):
        pl.semaphore_signal(barrier, inc=1, device_id=(lax.rem(a + o, n_alpha), b), device_id_type=MESH)
    for peer in (along(FAR), along(-FAR), along(-2), up, down, other):
        pl.semaphore_signal(barrier, inc=1, device_id=(a, peer), device_id_type=MESH)

    per = BLK // cap
    row_ids = lax.broadcasted_iota(I32, (BLK, BLK), 0)
    local = coeffs[...]
    for g in range(slots // BLK):
        line = jnp.concatenate([send_rows[g * per + k : g * per + k + 1, :] for k in range(per)], axis=1)
        cut = slice(g * BLK, (g + 1) * BLK)
        hot[cut, :] = jnp.where(row_ids == line, 1.0, 0.0).T.astype(BF16)
        picked[cut, :] = jnp.dot(hot[cut, :], local, preferred_element_type=F32).astype(BF16)

    src_t[...] = a_source[...].astype(F32).T
    sgn_t[...] = a_sign[...].astype(F32).T
    r16 = lax.broadcasted_iota(I32, (2 * NP, n_pairs), 0)
    c16 = lax.broadcasted_iota(I32, (2 * NP, n_pairs), 1)
    want = jnp.where(r16 < NP, b * NP + r16, other * NP + r16 - NP)
    v16[...] = jnp.dot(
        jnp.where(c16 == want, 1.0, 0.0).astype(BF16), integrals[...], preferred_element_type=F32).astype(BF16)
    pair_at = lax.broadcasted_iota(I32, (NP, BLK), 0) * (2 * cols) + LEAD
    pair_at = pair_at - lax.rem(lax.broadcasted_iota(I32, (NP, BLK), 1), 8)
    for c in range(cols // BLK):
        cut = slice(c * BLK, (c + 1) * BLK)
        idx_v[c] = b_source[:, cut] + jnp.where(b_sign[:, cut] < 0, cols, 0) + pair_at

    slot_ids = lax.broadcasted_iota(I32, (slots, n_pairs), 0).astype(F32)

    def weight_unit(unit):
        for k in range(UNIT):
            at = unit * UNIT + k
            line = pl.ds(core * HALF + at, 1)
            pick = jnp.where(slot_ids == src_t[line, :], sgn_t[line, :], 0.0).astype(BF16)
            w_raw[at] = lax.dot_general(v16[...], pick, (((1,), (1,)), ((), ())), preferred_element_type=F32)

    @pl.loop(0, units // 2)
    def _(unit):
        weight_unit(unit)

    pl.semaphore_wait(barrier, n_alpha - 1 + 6)

    def raw_copy(j):
        away = (FAR, -FAR, 1, 2, -1)[j]
        return pltpu.make_async_remote_copy(
            src_ref=(coeffs, coeffs, raw.at[0], raw.at[0], raw.at[1])[j], dst_ref=raw.at[j],
            send_sem=raw_send.at[j], recv_sem=raw_recv.at[j], device_id=(a, along(away)), device_id_type=MESH)

    for j in range(2):
        raw_copy(j).start()

    def pick_copy(to, frm):
        return pltpu.make_async_remote_copy(
            src_ref=picked.at[pl.ds(pl.multiple_of(to * cap, cap), cap), :],
            dst_ref=received.at[pl.ds(pl.multiple_of(frm * cap, cap), cap), :],
            send_sem=pick_send.at[to], recv_sem=pick_recv.at[frm],
            device_id=(to, b), device_id_type=MESH)

    @pl.loop(1, n_alpha)
    def _(o):
        pick_copy(lax.rem(a + o, n_alpha), a).start()

    mine = pl.ds(pl.multiple_of(a * cap, cap), cap)
    received[mine, :] = picked[mine, :]

    def half_rows(h):
        return pl.ds(pl.multiple_of(h * HALF, HALF), HALF)

    def w_copy():
        return pltpu.make_async_remote_copy(
            src_ref=w_out, dst_ref=w_full.at[:, half_rows(core), :],
            send_sem=w_send, recv_sem=w_recv, device_id=(a, other), device_id_type=MESH)

    def w_wait():
        return pltpu.make_async_remote_copy(
            src_ref=w_out, dst_ref=w_full.at[:, half_rows(1 - core), :],
            send_sem=w_send, recv_sem=w_recv, device_id=(a, other), device_id_type=MESH)

    @pl.loop(units // 2, units)
    def _(unit):
        weight_unit(unit)

    for p in range(NP):
        w_out[p] = w_raw[:, NP + p, :].astype(BF16)
    w_copy().start()
    for p in range(NP):
        w_full[p, half_rows(core), :] = w_raw[:, p, :].astype(BF16)

    for j in range(2):
        raw_copy(j).wait_recv()
    for j in range(2, 5):
        raw_copy(j).start()

    @pl.loop(1, n_alpha)
    def _(o):
        pick_copy(a, lax.rem(a + o, n_alpha)).wait_recv()

    table[b] = received[...].astype(F32).T.astype(BF16)

    def origin_of(n):
        s = (n + 1) // 2
        away = jnp.where(n % 2 == 1, -s, s)
        for j, far in enumerate((-FAR, FAR, -FAR - 1, -FAR - 2, FAR + 1)):
            away = jnp.where(n == 2 * HOPS + 1 + j, far, away)
        return lax.rem(z + away + n_z, n_z)

    def ring_copy(m, origin, d, h):
        ref = table.at[origin * 2 + core, pl.ds(pl.multiple_of(h * PART, PART), PART), :]
        return pltpu.make_async_remote_copy(
            src_ref=ref, dst_ref=ref, send_sem=ring_send.at[m], recv_sem=ring_recv.at[m],
            device_id=(a, jnp.where(d == 0, up, down)), device_id_type=MESH)

    def half_copy(n, h, origin, who):
        ref = table.at[origin * 2 + who, half_rows(h), :]
        return pltpu.make_async_remote_copy(
            src_ref=ref, dst_ref=ref, send_sem=half_send.at[n * 2 + h], recv_sem=half_recv.at[n * 2 + h],
            device_id=(a, other), device_id_type=MESH)

    for h in range(PARTS):
        for d in range(2):
            ring_copy(h * 2 + d, z, d, h).start()
    for h in range(2):
        half_copy(0, h, z, core).start()

    def far_copy(g, to, frm):
        low, count = GROUPS[g]
        return pltpu.make_async_remote_copy(
            src_ref=far_picked.at[pl.ds(low, count), pl.ds(pl.multiple_of(to * cap, cap), cap), :],
            dst_ref=far_received.at[pl.ds(low, count), pl.ds(pl.multiple_of(frm * cap, cap), cap), :],
            send_sem=far_send.at[g * n_alpha + to], recv_sem=far_recv.at[g * n_alpha + frm],
            device_id=(to, b), device_id_type=MESH)

    def far_pick(g):
        low, count = GROUPS[g]
        for j in range(low, low + count):
            far_picked[j] = jnp.dot(hot[...], raw[j], preferred_element_type=F32).astype(BF16)

        @pl.loop(1, n_alpha)
        def _(o):
            far_copy(g, lax.rem(a + o, n_alpha), a).start()

        for j in range(low, low + count):
            far_received[j, mine, :] = far_picked[j, mine, :]

    def far_wait(g):
        @pl.loop(1, n_alpha)
        def _(o):
            far_copy(g, a, lax.rem(a + o, n_alpha)).wait_recv()

    def far_turn(j):
        n = 2 * HOPS + 1 + j
        origin = origin_of(n)
        table[origin * 2 + core] = far_received[j].astype(F32).T.astype(BF16)
        for h in range(2):
            half_copy(n, h, origin, core).start()

    def mix(k):
        n = jnp.where(k == 7, 11, jnp.where(k == 10, 12, jnp.where(k < 7, k, jnp.where(k < 10, k - 1, k - 2))))
        n = jnp.where(k > 12, k, n)
        origin = origin_of(n)
        for h in range(2):
            half_copy(n, h, origin, 1 - core).wait_recv()
        rows = table[pl.ds(origin * 2, 2)].reshape(2 * BLK, slots)
        for p in range(0, NP, 2):
            r = jnp.dot(rows, w_t[:, p * BLK : (p + 2) * BLK], preferred_element_type=F32)
            for k in range(2):
                at = LEAD + (p + k) * 2 * cols + origin * (2 * BLK)
                x = r[:, k * BLK : (k + 1) * BLK]
                big[pl.ds(pl.multiple_of(at, 8), 2 * BLK), :] = x
                big[pl.ds(pl.multiple_of(at + cols, 8), 2 * BLK), :] = -x

    far_pick(0)
    w_wait().wait_recv()
    for p in range(NP):
        w_t[:, p * BLK : (p + 1) * BLK] = w_full[p].astype(F32).T.astype(BF16)

    def target(s):
        return jnp.maximum(jnp.maximum(2 * s - 1, 3 * s - 4), 0)

    @pl.loop(0, ROUND * HOPS)
    def _(m):
        s, d, h = m // ROUND + 1, m % 2, (m % ROUND) // 2
        origin = lax.rem(jnp.where(d == 0, z - s, z + s) + n_z, n_z)
        ring_copy(m, origin, d, h).wait_recv()

        @pl.when(s < HOPS)
        def _():
            ring_copy(m + ROUND, origin, d, h).start()

        @pl.when(h % 2 == 1)
        def _():
            half_copy(2 * s - 1 + d, h // 2, origin, core).start()

        @pl.when(m == ROUND - 1)
        def _():
            for j in range(2, 5):
                raw_copy(j).wait_recv()
            far_pick(1)

        low, high = target(s - 1), target(s)
        k = m % ROUND

        @pl.loop(low + ((high - low) * k) // ROUND, low + ((high - low) * (k + 1)) // ROUND)
        def _(n):
            mix(n)

        @pl.when(m == 3 * ROUND - 1)
        def _():
            far_wait(0)
            far_turn(0)

        @pl.when(m == 4 * ROUND - 1)
        def _():
            far_turn(1)

    side = jnp.where(z % 2 == 1, 1, -1)
    mate = lax.rem(z - side + n_z, n_z)

    def owner_of(i):
        far = steps - 1 - i // 2
        return lax.rem(jnp.where(i % 2 == 1, z + side * far, mate - side * far) + n_z, n_z)

    def idx_copy(i, which):
        chunk = owner_of(i) * 2 + jnp.where(which == 0, 1 - core, core)
        return pltpu.make_async_copy(idx_v.at[chunk], idx_s.at[which], idx_sem.at[which])

    for which in range(2):
        idx_copy(0, which).start()

    far_wait(1)
    for j in range(2, 5):
        far_turn(j)

    @pl.loop(3 * HOPS - 4, n_z)
    def _(n):
        mix(n)

    sub = lax.broadcasted_iota(I32, (8, BLK), 0)

    def gather(which, dst):
        for u in range(BLK // 8):
            total = None
            for k in range(8):
                acc = None
                for p in range(NP):
                    v = big[pl.ds(idx_s[which, p, u * 8 + k], 8), :]
                    acc = v if acc is None else acc + v
                total = acc if total is None else jnp.where(sub == k, acc, total)
            dst[u * 8 : (u + 1) * 8, :] = total

    def sib_copy(i):
        return pltpu.make_async_remote_copy(
            src_ref=sib_out.at[i], dst_ref=sib_in.at[i], send_sem=sib_send.at[i], recv_sem=sib_recv.at[i],
            device_id=(a, other), device_id_type=MESH)

    def mate_copy(t):
        return pltpu.make_async_remote_copy(
            src_ref=mate_out.at[t], dst_ref=mate_in.at[t], send_sem=mate_send.at[t], recv_sem=mate_recv.at[t],
            device_id=(a, mate * 2 + core), device_id_type=MESH)

    def rs_copy(t):
        return pltpu.make_async_remote_copy(
            src_ref=rs_out.at[t], dst_ref=rs_in.at[t], send_sem=rs_send.at[t], recv_sem=rs_recv.at[t],
            device_id=(a, owner_of(2 * t + 1) * 2 + core), device_id_type=MESH)

    def pass_on(t):
        mate_copy(t).wait_recv()
        rs_out[t] = (terms[2 * t + 1] + mate_in[t].astype(F32)).astype(BF16)
        rs_copy(t).start()

    def chip_sum(i):
        sib_copy(i).wait_recv()
        terms[i] = terms[i] + sib_in[i]

        @pl.when(i % 2 == 0)
        def _():
            mate_out[i // 2] = terms[i].astype(BF16)
            mate_copy(i // 2).start()

    @pl.loop(0, n_z)
    def _(i):
        idx_copy(i, 0).wait()
        gather(0, sib_out.at[i])
        sib_copy(i).start()

        @pl.when(i + 1 < n_z)
        def _():
            idx_copy(i + 1, 0).start()

        @pl.when(i > 0)
        def _():
            chip_sum(i - 1)

        @pl.when(jnp.logical_and(i % 2 == 1, i >= LAG))
        def _():
            pass_on((i - LAG) // 2)

        idx_copy(i, 1).wait()
        gather(1, terms.at[i])

        @pl.when(i + 1 < n_z)
        def _():
            idx_copy(i + 1, 1).start()

    last = n_z - 1
    for t in range((last - LAG) // 2 + 1, steps - 1):
        pass_on(t)
    @pl.loop(1, n_alpha)
    def _(o):
        pick_copy(lax.rem(a + o, n_alpha), a).wait_send()

        for g in range(2):
            far_copy(g, lax.rem(a + o, n_alpha), a).wait_send()

    for j in range(5):
        raw_copy(j).wait_send()

    @pl.loop(0, ROUND * HOPS)
    def _(m):
        ring_copy(m, z, m % 2, (m % ROUND) // 2).wait_send()

    @pl.loop(0, 2 * n_z)
    def _(j):
        half_copy(j // 2, j % 2, z, core).wait_send()

    w_copy().wait_send()

    @pl.loop(0, n_z)
    def _(i):
        sib_copy(i).wait_send()

    @pl.loop(0, steps)
    def _(t):
        mate_copy(t).wait_send()

        @pl.when(t < steps - 1)
        def _():
            rs_copy(t).wait_send()

    chip_sum(last)
    mate_copy(steps - 1).wait_recv()
    total = terms[last] + mate_in[steps - 1].astype(F32)
    for t in range(steps - 1):
        rs_copy(t).wait_recv()
        total = total + rs_in[t].astype(F32)
    out[...] = total.T.astype(BF16)


def body(n_alpha, n_z, coeffs, send_rows, a_source, a_sign, b_source, b_sign, integrals):
    cap = send_rows.shape[1]
    slots = n_alpha * cap
    n_pairs = integrals.shape[0]
    cols = b_source.shape[1]
    V, DMA = pltpu.VMEM, pltpu.SemaphoreType.DMA
    blocks, half = 2 * n_z, n_z // 2
    scratch = [
        V((slots, BLK), BF16), V((slots, BLK), BF16), V((slots, BLK), BF16),
        V((5, BLK, BLK), BF16), V((5, slots, BLK), BF16), V((5, slots, BLK), BF16), V((blocks, BLK, slots), BF16),
        V((BLK, n_pairs), F32), V((BLK, n_pairs), F32), V((2 * NP, n_pairs), BF16),
        V((HALF, 2 * NP, slots), F32), V((NP, HALF, slots), BF16), V((NP, BLK, slots), BF16),
        V((slots, NP * BLK), BF16), V((NP * 2 * cols + 2 * LEAD, BLK), F32),
        V((cols // BLK, NP, BLK), I32), pltpu.SMEM((2, NP, BLK), I32),
        V((half, BLK, BLK), BF16), V((half, BLK, BLK), BF16), V((half, BLK, BLK), BF16), V((half, BLK, BLK), BF16),
        V((n_z, BLK, BLK), F32), V((n_z, BLK, BLK), F32), V((n_z, BLK, BLK), F32),
        DMA((n_alpha,)), DMA((n_alpha,)), DMA((5,)), DMA((5,)), DMA((2 * n_alpha,)), DMA((2 * n_alpha,)),
        DMA((ROUND * HOPS,)), DMA((ROUND * HOPS,)),
        DMA((2 * n_z,)), DMA((2 * n_z,)),
        DMA, DMA, DMA((half,)), DMA((half,)), DMA((half,)), DMA((half,)), DMA((n_z,)), DMA((n_z,)), DMA((2,)),
    ]
    return pl.pallas_call(
        functools.partial(kernel, n_alpha, n_z),
        out_shape=jax.ShapeDtypeStruct((BLK, BLK), BF16),
        in_specs=[pl.BlockSpec(memory_space=V)] * 7,
        out_specs=pl.BlockSpec(memory_space=V),
        scratch_shapes=scratch,
        compiler_params=pltpu.CompilerParams(
            collective_id=0, has_side_effects=True, vmem_limit_bytes=60 * 2**20),
    )(coeffs, send_rows, a_source, a_sign, b_source, b_sign, integrals)


def solution(mesh):
    in_specs = (
        P("alpha", "beta"), P("alpha", None), P(None, "alpha"), P(None, "alpha"),
        P("beta", None), P("beta", None), P(),
    )
    run = functools.partial(body, mesh.shape["alpha"], mesh.shape["beta"] // 2)
    return jax.shard_map(run, mesh=mesh, in_specs=in_specs, out_specs=P("alpha", "beta"), check_vma=False)
```

```python
import functools

import jax
import jax.numpy as jnp
from jax import lax
from jax.experimental import pallas as pl
from jax.experimental.pallas import tpu as pltpu
from jax.sharding import PartitionSpec as P

MESH = pl.DeviceIdType.MESH
BF16, F32, I32 = jnp.bfloat16, jnp.float32, jnp.int32
BLK = 128
NP = 8
HALF = 64
PARTS = 4
PART = BLK // PARTS
ROUND = 2 * PARTS
UNIT = 4
LEAD = 8
LAG = 5
HOPS = 5
FAR = 6
GROUPS = ((0, 2), (2, 3))


def kernel(
    n_alpha, n_z,
    coeffs_hbm, send_rows_hbm, a_source_hbm, a_sign_hbm, b_source_hbm, b_sign_hbm, integrals_hbm,
    out,
    coeffs, send_rows, a_source, a_sign, b_source, b_sign, integrals,
    picked, received, hot, raw, far_picked, far_received, table, src_t, sgn_t, v16, w_raw, w_out, w_full, w_t, big, idx_v, idx_s,
    rs_in, rs_out, mate_in, mate_out, terms, sib_in, sib_out,
    pick_send, pick_recv, raw_send, raw_recv, far_send, far_recv, ring_send, ring_recv, half_send, half_recv, w_send, w_recv,
    rs_send, rs_recv, mate_send, mate_recv, sib_send, sib_recv, idx_sem, load_sem,
):
    a = lax.axis_index("alpha")
    b = lax.axis_index("beta")
    z, core = b // 2, b % 2
    cap = send_rows.shape[1]
    slots = n_alpha * cap
    n_pairs = integrals.shape[0]
    cols = b_source.shape[1]
    steps = n_z // 2
    units = HALF // UNIT

    def along(away):
        return lax.rem(z + away + n_z, n_z) * 2 + core

    up, down = along(1), along(-1)
    other = z * 2 + 1 - core

    barrier = pltpu.get_barrier_semaphore()
    for peer in (along(FAR), along(-FAR)):
        pl.semaphore_signal(barrier, inc=1, device_id=(a, peer), device_id_type=MESH)
    for o in range(1, n_alpha):
        pl.semaphore_signal(barrier, inc=1, device_id=(lax.rem(a + o, n_alpha), b), device_id_type=MESH)
    for peer in (along(-2), up, down, other):
        pl.semaphore_signal(barrier, inc=1, device_id=(a, peer), device_id_type=MESH)

    given = (
        (send_rows_hbm, send_rows), (coeffs_hbm, coeffs), (a_source_hbm, a_source), (a_sign_hbm, a_sign),
        (integrals_hbm, integrals), (b_source_hbm, b_source), (b_sign_hbm, b_sign))
    loads = [pltpu.make_async_copy(src, dst, load_sem.at[k]) for k, (src, dst) in enumerate(given)]
    for load in loads:
        load.start()

    for load in loads[:2]:
        load.wait()
    per = BLK // cap
    row_ids = lax.broadcasted_iota(I32, (BLK, BLK), 0)
    local = coeffs[...]
    for g in range(slots // BLK):
        line = jnp.concatenate([send_rows[g * per + k : g * per + k + 1, :] for k in range(per)], axis=1)
        cut = slice(g * BLK, (g + 1) * BLK)
        hot[cut, :] = jnp.where(row_ids == line, 1.0, 0.0).T.astype(BF16)
        picked[cut, :] = jnp.dot(hot[cut, :], local, preferred_element_type=F32).astype(BF16)

    for load in loads[2:]:
        load.wait()
    src_t[...] = a_source[...].astype(F32).T
    sgn_t[...] = a_sign[...].astype(F32).T
    r16 = lax.broadcasted_iota(I32, (2 * NP, n_pairs), 0)
    c16 = lax.broadcasted_iota(I32, (2 * NP, n_pairs), 1)
    want = jnp.where(r16 < NP, b * NP + r16, other * NP + r16 - NP)
    v16[...] = jnp.dot(
        jnp.where(c16 == want, 1.0, 0.0).astype(BF16), integrals[...], preferred_element_type=F32).astype(BF16)
    pair_at = lax.broadcasted_iota(I32, (NP, BLK), 0) * (2 * cols) + LEAD
    pair_at = pair_at - lax.rem(lax.broadcasted_iota(I32, (NP, BLK), 1), 8)
    for c in range(cols // BLK):
        cut = slice(c * BLK, (c + 1) * BLK)
        idx_v[c] = b_source[:, cut] + jnp.where(b_sign[:, cut] < 0, cols, 0) + pair_at

    slot_ids = lax.broadcasted_iota(I32, (slots, n_pairs), 0).astype(F32)

    def weight_unit(unit):
        for k in range(UNIT):
            at = unit * UNIT + k
            line = pl.ds(core * HALF + at, 1)
            pick = jnp.where(slot_ids == src_t[line, :], sgn_t[line, :], 0.0).astype(BF16)
            w_raw[at] = lax.dot_general(v16[...], pick, (((1,), (1,)), ((), ())), preferred_element_type=F32)

    @pl.loop(0, units // 2)
    def _(unit):
        weight_unit(unit)

    pl.semaphore_wait(barrier, n_alpha - 1 + 6)

    def raw_copy(j):
        away = (FAR, -FAR, 1, 2, -1)[j]
        return pltpu.make_async_remote_copy(
            src_ref=(coeffs, coeffs, raw.at[0], raw.at[0], raw.at[1])[j], dst_ref=raw.at[j],
            send_sem=raw_send.at[j], recv_sem=raw_recv.at[j], device_id=(a, along(away)), device_id_type=MESH)

    for j in range(2):
        raw_copy(j).start()

    def pick_copy(to, frm):
        return pltpu.make_async_remote_copy(
            src_ref=picked.at[pl.ds(pl.multiple_of(to * cap, cap), cap), :],
            dst_ref=received.at[pl.ds(pl.multiple_of(frm * cap, cap), cap), :],
            send_sem=pick_send.at[to], recv_sem=pick_recv.at[frm],
            device_id=(to, b), device_id_type=MESH)

    @pl.loop(1, n_alpha)
    def _(o):
        pick_copy(lax.rem(a + o, n_alpha), a).start()

    mine = pl.ds(pl.multiple_of(a * cap, cap), cap)
    received[mine, :] = picked[mine, :]

    def half_rows(h):
        return pl.ds(pl.multiple_of(h * HALF, HALF), HALF)

    def w_copy():
        return pltpu.make_async_remote_copy(
            src_ref=w_out, dst_ref=w_full.at[:, half_rows(core), :],
            send_sem=w_send, recv_sem=w_recv, device_id=(a, other), device_id_type=MESH)

    def w_wait():
        return pltpu.make_async_remote_copy(
            src_ref=w_out, dst_ref=w_full.at[:, half_rows(1 - core), :],
            send_sem=w_send, recv_sem=w_recv, device_id=(a, other), device_id_type=MESH)

    @pl.loop(units // 2, units)
    def _(unit):
        weight_unit(unit)

    for p in range(NP):
        w_out[p] = w_raw[:, NP + p, :].astype(BF16)
    w_copy().start()
    for p in range(NP):
        w_full[p, half_rows(core), :] = w_raw[:, p, :].astype(BF16)

    for j in range(2):
        raw_copy(j).wait_recv()
    for j in range(2, 5):
        raw_copy(j).start()

    @pl.loop(1, n_alpha)
    def _(o):
        pick_copy(a, lax.rem(a + o, n_alpha)).wait_recv()

    table[b] = received[...].astype(F32).T.astype(BF16)

    def origin_of(n):
        s = (n + 1) // 2
        away = jnp.where(n % 2 == 1, -s, s)
        for j, far in enumerate((-FAR, FAR, -FAR - 1, -FAR - 2, FAR + 1)):
            away = jnp.where(n == 2 * HOPS + 1 + j, far, away)
        return lax.rem(z + away + n_z, n_z)

    def ring_copy(m, origin, d, h):
        ref = table.at[origin * 2 + core, pl.ds(pl.multiple_of(h * PART, PART), PART), :]
        return pltpu.make_async_remote_copy(
            src_ref=ref, dst_ref=ref, send_sem=ring_send.at[m], recv_sem=ring_recv.at[m],
            device_id=(a, jnp.where(d == 0, up, down)), device_id_type=MESH)

    def half_copy(n, h, origin, who):
        ref = table.at[origin * 2 + who, half_rows(h), :]
        return pltpu.make_async_remote_copy(
            src_ref=ref, dst_ref=ref, send_sem=half_send.at[n * 2 + h], recv_sem=half_recv.at[n * 2 + h],
            device_id=(a, other), device_id_type=MESH)

    for h in range(PARTS):
        for d in range(2):
            ring_copy(h * 2 + d, z, d, h).start()
    for h in range(2):
        half_copy(0, h, z, core).start()

    def far_copy(g, to, frm):
        low, count = GROUPS[g]
        return pltpu.make_async_remote_copy(
            src_ref=far_picked.at[pl.ds(low, count), pl.ds(pl.multiple_of(to * cap, cap), cap), :],
            dst_ref=far_received.at[pl.ds(low, count), pl.ds(pl.multiple_of(frm * cap, cap), cap), :],
            send_sem=far_send.at[g * n_alpha + to], recv_sem=far_recv.at[g * n_alpha + frm],
            device_id=(to, b), device_id_type=MESH)

    def far_pick(g):
        low, count = GROUPS[g]
        for j in range(low, low + count):
            far_picked[j] = jnp.dot(hot[...], raw[j], preferred_element_type=F32).astype(BF16)

        @pl.loop(1, n_alpha)
        def _(o):
            far_copy(g, lax.rem(a + o, n_alpha), a).start()

        for j in range(low, low + count):
            far_received[j, mine, :] = far_picked[j, mine, :]

    def far_wait(g):
        @pl.loop(1, n_alpha)
        def _(o):
            far_copy(g, a, lax.rem(a + o, n_alpha)).wait_recv()

    def far_turn(j):
        n = 2 * HOPS + 1 + j
        origin = origin_of(n)
        table[origin * 2 + core] = far_received[j].astype(F32).T.astype(BF16)
        for h in range(2):
            half_copy(n, h, origin, core).start()

    def mix(k):
        n = jnp.where(k == 7, 11, jnp.where(k == 10, 12, jnp.where(k < 7, k, jnp.where(k < 10, k - 1, k - 2))))
        n = jnp.where(k > 12, k, n)
        origin = origin_of(n)
        for h in range(2):
            half_copy(n, h, origin, 1 - core).wait_recv()
        rows = table[pl.ds(origin * 2, 2)].reshape(2 * BLK, slots)
        for p in range(0, NP, 2):
            r = jnp.dot(rows, w_t[:, p * BLK : (p + 2) * BLK], preferred_element_type=F32)
            for k in range(2):
                at = LEAD + (p + k) * 2 * cols + origin * (2 * BLK)
                x = r[:, k * BLK : (k + 1) * BLK]
                big[pl.ds(pl.multiple_of(at, 8), 2 * BLK), :] = x
                big[pl.ds(pl.multiple_of(at + cols, 8), 2 * BLK), :] = -x

    far_pick(0)
    w_wait().wait_recv()
    for p in range(NP):
        w_t[:, p * BLK : (p + 1) * BLK] = w_full[p].astype(F32).T.astype(BF16)

    def target(s):
        return jnp.maximum(jnp.maximum(2 * s - 1, 3 * s - 4), 0)

    @pl.loop(0, ROUND * HOPS)
    def _(m):
        s, d, h = m // ROUND + 1, m % 2, (m % ROUND) // 2
        origin = lax.rem(jnp.where(d == 0, z - s, z + s) + n_z, n_z)
        ring_copy(m, origin, d, h).wait_recv()

        @pl.when(s < HOPS)
        def _():
            ring_copy(m + ROUND, origin, d, h).start()

        @pl.when(h % 2 == 1)
        def _():
            half_copy(2 * s - 1 + d, h // 2, origin, core).start()

        @pl.when(m == ROUND - 1)
        def _():
            for j in range(2, 5):
                raw_copy(j).wait_recv()
            far_pick(1)

        low, high = target(s - 1), target(s)
        k = m % ROUND

        @pl.loop(low + ((high - low) * k) // ROUND, low + ((high - low) * (k + 1)) // ROUND)
        def _(n):
            mix(n)

        @pl.when(m == 3 * ROUND - 1)
        def _():
            far_wait(0)
            far_turn(0)

        @pl.when(m == 4 * ROUND - 1)
        def _():
            far_turn(1)

        @pl.when(m == 4 * ROUND + 2)
        def _():
            far_wait(1)

        for j in range(2, 5):
            @pl.when(m == 4 * ROUND + 1 + j)
            def _(j=j):
                far_turn(j)

    side = jnp.where(z % 2 == 1, 1, -1)
    mate = lax.rem(z - side + n_z, n_z)

    def owner_of(i):
        far = steps - 1 - i // 2
        return lax.rem(jnp.where(i % 2 == 1, z + side * far, mate - side * far) + n_z, n_z)

    def idx_copy(i, which):
        chunk = owner_of(i) * 2 + jnp.where(which == 0, 1 - core, core)
        return pltpu.make_async_copy(idx_v.at[chunk], idx_s.at[which], idx_sem.at[which])

    for which in range(2):
        idx_copy(0, which).start()

    @pl.loop(3 * HOPS - 4, n_z)
    def _(n):
        mix(n)

    sub = lax.broadcasted_iota(I32, (8, BLK), 0)

    def gather(which, dst):
        for u in range(BLK // 8):
            total = None
            for k in range(8):
                acc = None
                for p in range(NP):
                    v = big[pl.ds(idx_s[which, p, u * 8 + k], 8), :]
                    acc = v if acc is None else acc + v
                total = acc if total is None else jnp.where(sub == k, acc, total)
            dst[u * 8 : (u + 1) * 8, :] = total

    def sib_copy(i):
        return pltpu.make_async_remote_copy(
            src_ref=sib_out.at[i], dst_ref=sib_in.at[i], send_sem=sib_send.at[i], recv_sem=sib_recv.at[i],
            device_id=(a, other), device_id_type=MESH)

    def mate_copy(t):
        return pltpu.make_async_remote_copy(
            src_ref=mate_out.at[t], dst_ref=mate_in.at[t], send_sem=mate_send.at[t], recv_sem=mate_recv.at[t],
            device_id=(a, mate * 2 + core), device_id_type=MESH)

    def rs_copy(t):
        return pltpu.make_async_remote_copy(
            src_ref=rs_out.at[t], dst_ref=rs_in.at[t], send_sem=rs_send.at[t], recv_sem=rs_recv.at[t],
            device_id=(a, owner_of(2 * t + 1) * 2 + core), device_id_type=MESH)

    def pass_on(t):
        mate_copy(t).wait_recv()
        rs_out[t] = (terms[2 * t + 1] + mate_in[t].astype(F32)).astype(BF16)
        rs_copy(t).start()

    def chip_sum(i):
        sib_copy(i).wait_recv()
        terms[i] = terms[i] + sib_in[i]

        @pl.when(i % 2 == 0)
        def _():
            mate_out[i // 2] = terms[i].astype(BF16)
            mate_copy(i // 2).start()

    @pl.loop(0, n_z)
    def _(i):
        idx_copy(i, 0).wait()
        gather(0, sib_out.at[i])
        sib_copy(i).start()

        @pl.when(i + 1 < n_z)
        def _():
            idx_copy(i + 1, 0).start()

        @pl.when(i > 0)
        def _():
            chip_sum(i - 1)

        @pl.when(jnp.logical_and(i % 2 == 1, i >= LAG))
        def _():
            pass_on((i - LAG) // 2)

        idx_copy(i, 1).wait()
        gather(1, terms.at[i])

        @pl.when(i + 1 < n_z)
        def _():
            idx_copy(i + 1, 1).start()

    last = n_z - 1
    for t in range((last - LAG) // 2 + 1, steps - 1):
        pass_on(t)
    @pl.loop(1, n_alpha)
    def _(o):
        pick_copy(lax.rem(a + o, n_alpha), a).wait_send()

        for g in range(2):
            far_copy(g, lax.rem(a + o, n_alpha), a).wait_send()

    for j in range(5):
        raw_copy(j).wait_send()

    @pl.loop(0, ROUND * HOPS)
    def _(m):
        ring_copy(m, z, m % 2, (m % ROUND) // 2).wait_send()

    @pl.loop(0, 2 * n_z)
    def _(j):
        half_copy(j // 2, j % 2, z, core).wait_send()

    w_copy().wait_send()

    @pl.loop(0, n_z)
    def _(i):
        sib_copy(i).wait_send()

    @pl.loop(0, steps)
    def _(t):
        mate_copy(t).wait_send()

        @pl.when(t < steps - 1)
        def _():
            rs_copy(t).wait_send()

    chip_sum(last)
    mate_copy(steps - 1).wait_recv()
    total = terms[last] + mate_in[steps - 1].astype(F32)
    for t in range(steps - 1):
        rs_copy(t).wait_recv()
        total = total + rs_in[t].astype(F32)
    out[...] = total.T.astype(BF16)


def body(n_alpha, n_z, coeffs, send_rows, a_source, a_sign, b_source, b_sign, integrals):
    cap = send_rows.shape[1]
    slots = n_alpha * cap
    n_pairs = integrals.shape[0]
    cols = b_source.shape[1]
    V, DMA = pltpu.VMEM, pltpu.SemaphoreType.DMA
    blocks, half = 2 * n_z, n_z // 2
    scratch = [
        V((BLK, BLK), BF16), V(send_rows.shape, I32), V(a_source.shape, I32), V(a_sign.shape, I32),
        V(b_source.shape, I32), V(b_sign.shape, I32), V(integrals.shape, BF16),
        V((slots, BLK), BF16), V((slots, BLK), BF16), V((slots, BLK), BF16),
        V((5, BLK, BLK), BF16), V((5, slots, BLK), BF16), V((5, slots, BLK), BF16), V((blocks, BLK, slots), BF16),
        V((BLK, n_pairs), F32), V((BLK, n_pairs), F32), V((2 * NP, n_pairs), BF16),
        V((HALF, 2 * NP, slots), F32), V((NP, HALF, slots), BF16), V((NP, BLK, slots), BF16),
        V((slots, NP * BLK), BF16), V((NP * 2 * cols + 2 * LEAD, BLK), F32),
        V((cols // BLK, NP, BLK), I32), pltpu.SMEM((2, NP, BLK), I32),
        V((half, BLK, BLK), BF16), V((half, BLK, BLK), BF16), V((half, BLK, BLK), BF16), V((half, BLK, BLK), BF16),
        V((n_z, BLK, BLK), F32), V((n_z, BLK, BLK), F32), V((n_z, BLK, BLK), F32),
        DMA((n_alpha,)), DMA((n_alpha,)), DMA((5,)), DMA((5,)), DMA((2 * n_alpha,)), DMA((2 * n_alpha,)),
        DMA((ROUND * HOPS,)), DMA((ROUND * HOPS,)),
        DMA((2 * n_z,)), DMA((2 * n_z,)),
        DMA, DMA, DMA((half,)), DMA((half,)), DMA((half,)), DMA((half,)), DMA((n_z,)), DMA((n_z,)), DMA((2,)), DMA((7,)),
    ]
    return pl.pallas_call(
        functools.partial(kernel, n_alpha, n_z),
        out_shape=jax.ShapeDtypeStruct((BLK, BLK), BF16),
        in_specs=[pl.BlockSpec(memory_space=pl.ANY)] * 7,
        out_specs=pl.BlockSpec(memory_space=V),
        scratch_shapes=scratch,
        compiler_params=pltpu.CompilerParams(
            collective_id=0, has_side_effects=True, vmem_limit_bytes=60 * 2**20),
    )(coeffs, send_rows, a_source, a_sign, b_source, b_sign, integrals)


def solution(mesh):
    in_specs = (
        P("alpha", "beta"), P("alpha", None), P(None, "alpha"), P(None, "alpha"),
        P("beta", None), P("beta", None), P(),
    )
    run = functools.partial(body, mesh.shape["alpha"], mesh.shape["beta"] // 2)
    return jax.shard_map(run, mesh=mesh, in_specs=in_specs, out_specs=P("alpha", "beta"), check_vma=False)
```

```python
import functools
import math

import jax
import jax.numpy as jnp
from jax import lax
from jax.experimental import pallas as pl
from jax.experimental.pallas import tpu as pltpu
from jax.sharding import PartitionSpec as P

MESH = pl.DeviceIdType.MESH
BF16, F32, I32 = jnp.bfloat16, jnp.float32, jnp.int32
BLK = 128
NP = 8
HALF = 64
PARTS = 4
PART = BLK // PARTS
ROUND = 2 * PARTS
UNIT = 4
LEAD = 8
HOPS = 5
FAR = 6
GROUPS = ((0, 2), (2, 3))


def kernel(
    n_alpha, n_z,
    coeffs_hbm, send_rows_hbm, a_source_hbm, a_sign_hbm, b_source_hbm, b_sign_hbm, integrals_hbm,
    out,
    coeffs, send_rows, a_source, a_sign, b_source, b_sign, integrals,
    picked, received, hot, raw, far_picked, far_received, table, src_t, sgn_t, v16, w_raw, w_out, w_full, w_t, big, idx_v, idx_s,
    rs_in, rs_out, mate_in, mate_out, terms, sib_in, sib_out,
    pick_send, pick_recv, raw_send, raw_recv, far_send, far_recv, ring_send, ring_recv, half_send, half_recv, w_send, w_recv,
    rs_send, rs_recv, mate_send, mate_recv, sib_send, sib_recv, idx_sem, load_sem,
):
    a = lax.axis_index("alpha")
    b = lax.axis_index("beta")
    z, core = b // 2, b % 2
    cap = send_rows.shape[1]
    slots = n_alpha * cap
    n_pairs = integrals.shape[0]
    cols = b_source.shape[1]
    steps = n_z // 2
    units = HALF // UNIT

    def along(away):
        return lax.rem(z + away + n_z, n_z) * 2 + core

    up, down = along(1), along(-1)
    other = z * 2 + 1 - core

    barrier = pltpu.get_barrier_semaphore()
    for peer in (along(FAR), along(-FAR)):
        pl.semaphore_signal(barrier, inc=1, device_id=(a, peer), device_id_type=MESH)
    side_a = math.isqrt(n_alpha)
    offsets = [(dy, dx) for dy in range(side_a) for dx in range(side_a) if dy or dx]
    offsets.sort(key=lambda o: -sum(min(k, side_a - k) for k in o))
    peers = [lax.rem(a // side_a + dy, side_a) * side_a + lax.rem(a % side_a + dx, side_a) for dy, dx in offsets]
    for peer in peers:
        pl.semaphore_signal(barrier, inc=1, device_id=(peer, b), device_id_type=MESH)
    for peer in (along(-2), up, down, other):
        pl.semaphore_signal(barrier, inc=1, device_id=(a, peer), device_id_type=MESH)

    given = (
        (send_rows_hbm, send_rows), (coeffs_hbm, coeffs), (a_source_hbm, a_source), (a_sign_hbm, a_sign),
        (integrals_hbm, integrals), (b_source_hbm, b_source), (b_sign_hbm, b_sign))
    loads = [pltpu.make_async_copy(src, dst, load_sem.at[k]) for k, (src, dst) in enumerate(given)]
    for load in loads:
        load.start()

    for load in loads[:2]:
        load.wait()
    per = BLK // cap
    row_ids = lax.broadcasted_iota(I32, (BLK, BLK), 0)
    local = coeffs[...]
    for g in range(slots // BLK):
        line = jnp.concatenate([send_rows[g * per + k : g * per + k + 1, :] for k in range(per)], axis=1)
        cut = slice(g * BLK, (g + 1) * BLK)
        hot[cut, :] = jnp.where(row_ids == line, 1.0, 0.0).T.astype(BF16)
        picked[cut, :] = jnp.dot(hot[cut, :], local, preferred_element_type=F32).astype(BF16)

    for load in loads[2:]:
        load.wait()
    src_t[...] = a_source[...].astype(F32).T
    sgn_t[...] = a_sign[...].astype(F32).T
    r16 = lax.broadcasted_iota(I32, (2 * NP, n_pairs), 0)
    c16 = lax.broadcasted_iota(I32, (2 * NP, n_pairs), 1)
    want = jnp.where(r16 < NP, b * NP + r16, other * NP + r16 - NP)
    v16[...] = jnp.dot(
        jnp.where(c16 == want, 1.0, 0.0).astype(BF16), integrals[...], preferred_element_type=F32).astype(BF16)
    pair_at = lax.broadcasted_iota(I32, (NP, BLK), 0) * (2 * cols) + LEAD
    pair_at = pair_at - lax.rem(lax.broadcasted_iota(I32, (NP, BLK), 1), 8)
    for c in range(cols // BLK):
        cut = slice(c * BLK, (c + 1) * BLK)
        idx_v[c] = b_source[:, cut] + jnp.where(b_sign[:, cut] < 0, cols, 0) + pair_at

    slot_ids = lax.broadcasted_iota(I32, (slots, n_pairs), 0).astype(F32)

    def weight_unit(unit):
        for k in range(UNIT):
            at = unit * UNIT + k
            line = pl.ds(core * HALF + at, 1)
            pick = jnp.where(slot_ids == src_t[line, :], sgn_t[line, :], 0.0).astype(BF16)
            w_raw[at] = lax.dot_general(v16[...], pick, (((1,), (1,)), ((), ())), preferred_element_type=F32)

    @pl.loop(0, units // 2)
    def _(unit):
        weight_unit(unit)

    pl.semaphore_wait(barrier, n_alpha - 1 + 6)

    def raw_copy(j):
        away = (FAR, -FAR, 1, 2, -1)[j]
        return pltpu.make_async_remote_copy(
            src_ref=(coeffs, coeffs, raw.at[0], raw.at[0], raw.at[1])[j], dst_ref=raw.at[j],
            send_sem=raw_send.at[j], recv_sem=raw_recv.at[j], device_id=(a, along(away)), device_id_type=MESH)

    for j in range(2):
        raw_copy(j).start()

    def pick_copy(to, frm):
        return pltpu.make_async_remote_copy(
            src_ref=picked.at[pl.ds(pl.multiple_of(to * cap, cap), cap), :],
            dst_ref=received.at[pl.ds(pl.multiple_of(frm * cap, cap), cap), :],
            send_sem=pick_send.at[to], recv_sem=pick_recv.at[frm],
            device_id=(to, b), device_id_type=MESH)

    for peer in peers:
        pick_copy(peer, a).start()

    mine = pl.ds(pl.multiple_of(a * cap, cap), cap)
    received[mine, :] = picked[mine, :]

    def half_rows(h):
        return pl.ds(pl.multiple_of(h * HALF, HALF), HALF)

    def w_copy():
        return pltpu.make_async_remote_copy(
            src_ref=w_out, dst_ref=w_full.at[:, half_rows(core), :],
            send_sem=w_send, recv_sem=w_recv, device_id=(a, other), device_id_type=MESH)

    def w_wait():
        return pltpu.make_async_remote_copy(
            src_ref=w_out, dst_ref=w_full.at[:, half_rows(1 - core), :],
            send_sem=w_send, recv_sem=w_recv, device_id=(a, other), device_id_type=MESH)

    @pl.loop(units // 2, units)
    def _(unit):
        weight_unit(unit)

    for p in range(NP):
        w_out[p] = w_raw[:, NP + p, :].astype(BF16)
    w_copy().start()
    for p in range(NP):
        w_full[p, half_rows(core), :] = w_raw[:, p, :].astype(BF16)

    for j in range(2):
        raw_copy(j).wait_recv()
    for j in range(2, 5):
        raw_copy(j).start()

    @pl.loop(1, n_alpha)
    def _(o):
        pick_copy(a, lax.rem(a + o, n_alpha)).wait_recv()

    table[b] = received[...].astype(F32).T.astype(BF16)

    def origin_of(n):
        s = (n + 1) // 2
        away = jnp.where(n % 2 == 1, -s, s)
        for j, far in enumerate((-FAR, FAR, -FAR - 1, -FAR - 2, FAR + 1)):
            away = jnp.where(n == 2 * HOPS + 1 + j, far, away)
        return lax.rem(z + away + n_z, n_z)

    def ring_copy(m, origin, d, h):
        ref = table.at[origin * 2 + core, pl.ds(pl.multiple_of(h * PART, PART), PART), :]
        return pltpu.make_async_remote_copy(
            src_ref=ref, dst_ref=ref, send_sem=ring_send.at[m], recv_sem=ring_recv.at[m],
            device_id=(a, jnp.where(d == 0, up, down)), device_id_type=MESH)

    def half_copy(n, h, origin, who):
        ref = table.at[origin * 2 + who, half_rows(h), :]
        return pltpu.make_async_remote_copy(
            src_ref=ref, dst_ref=ref, send_sem=half_send.at[n * 2 + h], recv_sem=half_recv.at[n * 2 + h],
            device_id=(a, other), device_id_type=MESH)

    for h in range(PARTS):
        for d in range(2):
            ring_copy(h * 2 + d, z, d, h).start()
    for h in range(2):
        half_copy(0, h, z, core).start()

    def far_copy(g, to, frm):
        low, count = GROUPS[g]
        return pltpu.make_async_remote_copy(
            src_ref=far_picked.at[pl.ds(low, count), pl.ds(pl.multiple_of(to * cap, cap), cap), :],
            dst_ref=far_received.at[pl.ds(low, count), pl.ds(pl.multiple_of(frm * cap, cap), cap), :],
            send_sem=far_send.at[g * n_alpha + to], recv_sem=far_recv.at[g * n_alpha + frm],
            device_id=(to, b), device_id_type=MESH)

    def far_pick(g):
        low, count = GROUPS[g]
        for j in range(low, low + count):
            far_picked[j] = jnp.dot(hot[...], raw[j], preferred_element_type=F32).astype(BF16)

        @pl.loop(1, n_alpha)
        def _(o):
            far_copy(g, lax.rem(a + o, n_alpha), a).start()

        for j in range(low, low + count):
            far_received[j, mine, :] = far_picked[j, mine, :]

    def far_wait(g):
        @pl.loop(1, n_alpha)
        def _(o):
            far_copy(g, a, lax.rem(a + o, n_alpha)).wait_recv()

    def far_turn(j):
        n = 2 * HOPS + 1 + j
        origin = origin_of(n)
        table[origin * 2 + core] = far_received[j].astype(F32).T.astype(BF16)
        for h in range(2):
            half_copy(n, h, origin, core).start()

    def mix(k):
        n = jnp.where(k == 7, 11, jnp.where(k == 10, 12, jnp.where(k < 7, k, jnp.where(k < 10, k - 1, k - 2))))
        n = jnp.where(k > 12, k, n)
        origin = origin_of(n)
        for h in range(2):
            half_copy(n, h, origin, 1 - core).wait_recv()
        rows = table[pl.ds(origin * 2, 2)].reshape(2 * BLK, slots)
        for p in range(0, NP, 2):
            r = jnp.dot(rows, w_t[:, p * BLK : (p + 2) * BLK], preferred_element_type=F32)
            for k in range(2):
                at = LEAD + (p + k) * 2 * cols + origin * (2 * BLK)
                x = r[:, k * BLK : (k + 1) * BLK]
                big[pl.ds(pl.multiple_of(at, 8), 2 * BLK), :] = x
                big[pl.ds(pl.multiple_of(at + cols, 8), 2 * BLK), :] = -x

    far_pick(0)
    w_wait().wait_recv()
    for p in range(NP):
        w_t[:, p * BLK : (p + 1) * BLK] = w_full[p].astype(F32).T.astype(BF16)

    def target(s):
        return jnp.maximum(jnp.maximum(2 * s - 1, 3 * s - 4), 0)

    @pl.loop(0, ROUND * HOPS)
    def _(m):
        s, d, h = m // ROUND + 1, m % 2, (m % ROUND) // 2
        origin = lax.rem(jnp.where(d == 0, z - s, z + s) + n_z, n_z)
        ring_copy(m, origin, d, h).wait_recv()

        @pl.when(s < HOPS)
        def _():
            ring_copy(m + ROUND, origin, d, h).start()

        @pl.when(h % 2 == 1)
        def _():
            half_copy(2 * s - 1 + d, h // 2, origin, core).start()

        @pl.when(m == ROUND - 1)
        def _():
            for j in range(2, 5):
                raw_copy(j).wait_recv()
            far_pick(1)

        low, high = target(s - 1), target(s)
        k = m % ROUND

        @pl.loop(low + ((high - low) * k) // ROUND, low + ((high - low) * (k + 1)) // ROUND)
        def _(n):
            mix(n)

        @pl.when(m == 3 * ROUND - 1)
        def _():
            far_wait(0)
            far_turn(0)

        @pl.when(m == 4 * ROUND - 1)
        def _():
            far_turn(1)

        @pl.when(m == 4 * ROUND + 2)
        def _():
            far_wait(1)

        for j in range(2, 5):
            @pl.when(m == 4 * ROUND + 1 + j)
            def _(j=j):
                far_turn(j)

    side = jnp.where(z % 2 == 1, 1, -1)
    mate = lax.rem(z - side + n_z, n_z)

    last = n_z - 1

    def place(i):
        own = jnp.logical_or(jnp.logical_and(i % 2 == 1, i >= 3), i == last - 1)
        t_own = jnp.where(i >= last - 1, i - steps, (i - 3) // 2)
        return own, jnp.where(own, t_own, jnp.where(i < 3, i, i // 2 + 1))

    def owner_of(i):
        own, t = place(i)
        far = steps - 1 - t
        return lax.rem(jnp.where(own, z + side * far, mate - side * far) + n_z, n_z)

    def idx_copy(i, which):
        chunk = owner_of(i) * 2 + jnp.where(which == 0, 1 - core, core)
        return pltpu.make_async_copy(idx_v.at[chunk], idx_s.at[which], idx_sem.at[which])

    for which in range(2):
        idx_copy(0, which).start()

    @pl.loop(3 * HOPS - 4, n_z)
    def _(n):
        mix(n)

    sub = lax.broadcasted_iota(I32, (8, BLK), 0)

    def gather(which, dst):
        for u in range(BLK // 8):
            total = None
            for k in range(8):
                acc = None
                for p in range(NP):
                    v = big[pl.ds(idx_s[which, p, u * 8 + k], 8), :]
                    acc = v if acc is None else acc + v
                total = acc if total is None else jnp.where(sub == k, acc, total)
            dst[u * 8 : (u + 1) * 8, :] = total

    def sib_copy(i):
        return pltpu.make_async_remote_copy(
            src_ref=sib_out.at[i], dst_ref=sib_in.at[i], send_sem=sib_send.at[i], recv_sem=sib_recv.at[i],
            device_id=(a, other), device_id_type=MESH)

    def mate_copy(t):
        return pltpu.make_async_remote_copy(
            src_ref=mate_out.at[t], dst_ref=mate_in.at[t], send_sem=mate_send.at[t], recv_sem=mate_recv.at[t],
            device_id=(a, mate * 2 + core), device_id_type=MESH)

    def rs_copy(t):
        return pltpu.make_async_remote_copy(
            src_ref=rs_out.at[t], dst_ref=rs_in.at[t], send_sem=rs_send.at[t], recv_sem=rs_recv.at[t],
            device_id=(a, lax.rem(z + side * (steps - 1 - t) + n_z, n_z) * 2 + core), device_id_type=MESH)

    def chip_sum(i):
        sib_copy(i).wait_recv()
        terms[i] = terms[i] + sib_in[i]

        own, t = place(i)

        @pl.when(jnp.logical_not(own))
        def _():
            mate_out[t] = terms[i].astype(BF16)
            mate_copy(t).start()

        @pl.when(jnp.logical_and(own, i < last))
        def _():
            mate_copy(t).wait_recv()
            rs_out[t] = (terms[i] + mate_in[t].astype(F32)).astype(BF16)
            rs_copy(t).start()

    @pl.loop(0, n_z)
    def _(i):
        idx_copy(i, 0).wait()
        gather(0, sib_out.at[i])
        sib_copy(i).start()

        @pl.when(i + 1 < n_z)
        def _():
            idx_copy(i + 1, 0).start()

        @pl.when(i > 0)
        def _():
            chip_sum(i - 1)

        idx_copy(i, 1).wait()
        gather(1, terms.at[i])

        @pl.when(i + 1 < n_z)
        def _():
            idx_copy(i + 1, 1).start()

    @pl.loop(1, n_alpha)
    def _(o):
        pick_copy(lax.rem(a + o, n_alpha), a).wait_send()

        for g in range(2):
            far_copy(g, lax.rem(a + o, n_alpha), a).wait_send()

    for j in range(5):
        raw_copy(j).wait_send()

    @pl.loop(0, ROUND * HOPS)
    def _(m):
        ring_copy(m, z, m % 2, (m % ROUND) // 2).wait_send()

    @pl.loop(0, 2 * n_z)
    def _(j):
        half_copy(j // 2, j % 2, z, core).wait_send()

    w_copy().wait_send()

    @pl.loop(0, n_z)
    def _(i):
        sib_copy(i).wait_send()

    @pl.loop(0, steps)
    def _(t):
        mate_copy(t).wait_send()

        @pl.when(t < steps - 1)
        def _():
            rs_copy(t).wait_send()

    chip_sum(last)
    mate_copy(steps - 1).wait_recv()
    total = terms[last] + mate_in[steps - 1].astype(F32)
    for t in range(steps - 1):
        rs_copy(t).wait_recv()
        total = total + rs_in[t].astype(F32)
    out[...] = total.T.astype(BF16)


def body(n_alpha, n_z, coeffs, send_rows, a_source, a_sign, b_source, b_sign, integrals):
    cap = send_rows.shape[1]
    slots = n_alpha * cap
    n_pairs = integrals.shape[0]
    cols = b_source.shape[1]
    V, DMA = pltpu.VMEM, pltpu.SemaphoreType.DMA
    blocks, half = 2 * n_z, n_z // 2
    scratch = [
        V((BLK, BLK), BF16), V(send_rows.shape, I32), V(a_source.shape, I32), V(a_sign.shape, I32),
        V(b_source.shape, I32), V(b_sign.shape, I32), V(integrals.shape, BF16),
        V((slots, BLK), BF16), V((slots, BLK), BF16), V((slots, BLK), BF16),
        V((5, BLK, BLK), BF16), V((5, slots, BLK), BF16), V((5, slots, BLK), BF16), V((blocks, BLK, slots), BF16),
        V((BLK, n_pairs), F32), V((BLK, n_pairs), F32), V((2 * NP, n_pairs), BF16),
        V((HALF, 2 * NP, slots), F32), V((NP, HALF, slots), BF16), V((NP, BLK, slots), BF16),
        V((slots, NP * BLK), BF16), V((NP * 2 * cols + 2 * LEAD, BLK), F32),
        V((cols // BLK, NP, BLK), I32), pltpu.SMEM((2, NP, BLK), I32),
        V((half, BLK, BLK), BF16), V((half, BLK, BLK), BF16), V((half, BLK, BLK), BF16), V((half, BLK, BLK), BF16),
        V((n_z, BLK, BLK), F32), V((n_z, BLK, BLK), F32), V((n_z, BLK, BLK), F32),
        DMA((n_alpha,)), DMA((n_alpha,)), DMA((5,)), DMA((5,)), DMA((2 * n_alpha,)), DMA((2 * n_alpha,)),
        DMA((ROUND * HOPS,)), DMA((ROUND * HOPS,)),
        DMA((2 * n_z,)), DMA((2 * n_z,)),
        DMA, DMA, DMA((half,)), DMA((half,)), DMA((half,)), DMA((half,)), DMA((n_z,)), DMA((n_z,)), DMA((2,)), DMA((7,)),
    ]
    return pl.pallas_call(
        functools.partial(kernel, n_alpha, n_z),
        out_shape=jax.ShapeDtypeStruct((BLK, BLK), BF16),
        in_specs=[pl.BlockSpec(memory_space=pl.ANY)] * 7,
        out_specs=pl.BlockSpec(memory_space=V),
        scratch_shapes=scratch,
        compiler_params=pltpu.CompilerParams(
            collective_id=0, has_side_effects=True, vmem_limit_bytes=60 * 2**20),
    )(coeffs, send_rows, a_source, a_sign, b_source, b_sign, integrals)


def solution(mesh):
    in_specs = (
        P("alpha", "beta"), P("alpha", None), P(None, "alpha"), P(None, "alpha"),
        P("beta", None), P("beta", None), P(),
    )
    run = functools.partial(body, mesh.shape["alpha"], mesh.shape["beta"] // 2)
    return jax.shard_map(run, mesh=mesh, in_specs=in_specs, out_specs=P("alpha", "beta"), check_vma=False)
```

```python
import functools
import math

import jax
import jax.numpy as jnp
from jax import lax
from jax.experimental import pallas as pl
from jax.experimental.pallas import tpu as pltpu
from jax.sharding import PartitionSpec as P

MESH = pl.DeviceIdType.MESH
BF16, F32, I32 = jnp.bfloat16, jnp.float32, jnp.int32
BLK = 128
NP = 8
HALF = 64
PARTS = 4
PART = BLK // PARTS
ROUND = 2 * PARTS
UNIT = 4
LEAD = 8
HOPS = 5
FAR = 6
GROUPS = ((0, 2), (2, 3))


def kernel(
    n_alpha, n_z,
    coeffs_hbm, send_rows_hbm, a_source_hbm, a_sign_hbm, b_source_hbm, b_sign_hbm, integrals_hbm,
    out,
    coeffs, send_rows, a_source, a_sign, b_source, b_sign, integrals,
    picked, received, hot, raw, far_picked, far_received, table, src_t, sgn_t, v16, w_raw, w_out, w_full, w_t, big, idx_v, idx_s,
    rs_in, rs_out, mate_in, mate_out, terms, sib_in, sib_out,
    pick_send, pick_recv, raw_send, raw_recv, far_send, far_recv, ring_send, ring_recv, half_send, half_recv, w_send, w_recv,
    rs_send, rs_recv, mate_send, mate_recv, sib_send, sib_recv, idx_sem, load_sem,
):
    a = lax.axis_index("alpha")
    b = lax.axis_index("beta")
    z, core = b // 2, b % 2
    cap = send_rows.shape[1]
    slots = n_alpha * cap
    n_pairs = integrals.shape[0]
    cols = b_source.shape[1]
    steps = n_z // 2
    units = HALF // UNIT

    def along(away):
        return lax.rem(z + away + n_z, n_z) * 2 + core

    up, down = along(1), along(-1)
    other = z * 2 + 1 - core

    barrier = pltpu.get_barrier_semaphore()
    for peer in (along(FAR), along(-FAR)):
        pl.semaphore_signal(barrier, inc=1, device_id=(a, peer), device_id_type=MESH)
    side_a = math.isqrt(n_alpha)
    offsets = [(dy, dx) for dy in range(side_a) for dx in range(side_a) if dy or dx]
    offsets.sort(key=lambda o: -sum(min(k, side_a - k) for k in o))
    peers = [lax.rem(a // side_a + dy, side_a) * side_a + lax.rem(a % side_a + dx, side_a) for dy, dx in offsets]
    for peer in peers:
        pl.semaphore_signal(barrier, inc=1, device_id=(peer, b), device_id_type=MESH)
    for peer in (along(-2), up, down, other):
        pl.semaphore_signal(barrier, inc=1, device_id=(a, peer), device_id_type=MESH)

    given = (
        (send_rows_hbm, send_rows), (coeffs_hbm, coeffs), (a_source_hbm, a_source), (a_sign_hbm, a_sign),
        (integrals_hbm, integrals), (b_source_hbm, b_source), (b_sign_hbm, b_sign))
    loads = [pltpu.make_async_copy(src, dst, load_sem.at[k]) for k, (src, dst) in enumerate(given)]
    for load in loads:
        load.start()

    for load in loads[:2]:
        load.wait()
    per = BLK // cap
    row_ids = lax.broadcasted_iota(I32, (BLK, BLK), 0)
    local = coeffs[...]
    for g in range(slots // BLK):
        line = jnp.concatenate([send_rows[g * per + k : g * per + k + 1, :] for k in range(per)], axis=1)
        cut = slice(g * BLK, (g + 1) * BLK)
        hot[cut, :] = jnp.where(row_ids == line, 1.0, 0.0).T.astype(BF16)
        picked[cut, :] = jnp.dot(hot[cut, :], local, preferred_element_type=F32).astype(BF16)

    for load in loads[2:]:
        load.wait()
    src_t[...] = a_source[...].astype(F32).T
    sgn_t[...] = a_sign[...].astype(F32).T
    r16 = lax.broadcasted_iota(I32, (2 * NP, n_pairs), 0)
    c16 = lax.broadcasted_iota(I32, (2 * NP, n_pairs), 1)
    want = jnp.where(r16 < NP, b * NP + r16, other * NP + r16 - NP)
    v16[...] = jnp.dot(
        jnp.where(c16 == want, 1.0, 0.0).astype(BF16), integrals[...], preferred_element_type=F32).astype(BF16)
    pair_at = lax.broadcasted_iota(I32, (NP, BLK), 0) * (2 * cols) + LEAD
    pair_at = pair_at - lax.rem(lax.broadcasted_iota(I32, (NP, BLK), 1), 8)
    for c in range(cols // BLK):
        cut = slice(c * BLK, (c + 1) * BLK)
        idx_v[c] = b_source[:, cut] + jnp.where(b_sign[:, cut] < 0, cols, 0) + pair_at

    slot_ids = lax.broadcasted_iota(I32, (slots, n_pairs), 0).astype(F32)

    def weight_unit(unit):
        for k in range(UNIT):
            at = unit * UNIT + k
            line = pl.ds(core * HALF + at, 1)
            pick = jnp.where(slot_ids == src_t[line, :], sgn_t[line, :], 0.0).astype(BF16)
            w_raw[at] = lax.dot_general(v16[...], pick, (((1,), (1,)), ((), ())), preferred_element_type=F32)

    @pl.loop(0, units // 2)
    def _(unit):
        weight_unit(unit)

    pl.semaphore_wait(barrier, n_alpha - 1 + 6)

    def raw_copy(j):
        away = (FAR, -FAR, 1, 2, -1)[j]
        return pltpu.make_async_remote_copy(
            src_ref=(coeffs, coeffs, raw.at[0], raw.at[0], raw.at[1])[j], dst_ref=raw.at[j],
            send_sem=raw_send.at[j], recv_sem=raw_recv.at[j], device_id=(a, along(away)), device_id_type=MESH)

    for j in range(2):
        raw_copy(j).start()

    def pick_copy(to, frm):
        return pltpu.make_async_remote_copy(
            src_ref=picked.at[pl.ds(pl.multiple_of(to * cap, cap), cap), :],
            dst_ref=received.at[pl.ds(pl.multiple_of(frm * cap, cap), cap), :],
            send_sem=pick_send.at[to], recv_sem=pick_recv.at[frm],
            device_id=(to, b), device_id_type=MESH)

    for peer in peers:
        pick_copy(peer, a).start()

    mine = pl.ds(pl.multiple_of(a * cap, cap), cap)
    received[mine, :] = picked[mine, :]

    def half_rows(h):
        return pl.ds(pl.multiple_of(h * HALF, HALF), HALF)

    def w_copy():
        return pltpu.make_async_remote_copy(
            src_ref=w_out, dst_ref=w_full.at[:, half_rows(core), :],
            send_sem=w_send, recv_sem=w_recv, device_id=(a, other), device_id_type=MESH)

    def w_wait():
        return pltpu.make_async_remote_copy(
            src_ref=w_out, dst_ref=w_full.at[:, half_rows(1 - core), :],
            send_sem=w_send, recv_sem=w_recv, device_id=(a, other), device_id_type=MESH)

    @pl.loop(units // 2, units)
    def _(unit):
        weight_unit(unit)

    for p in range(NP):
        w_out[p] = w_raw[:, NP + p, :].astype(BF16)
    w_copy().start()
    for p in range(NP):
        w_full[p, half_rows(core), :] = w_raw[:, p, :].astype(BF16)

    for j in range(2):
        raw_copy(j).wait_recv()
    for j in range(2, 5):
        raw_copy(j).start()

    @pl.loop(1, n_alpha)
    def _(o):
        pick_copy(a, lax.rem(a + o, n_alpha)).wait_recv()

    table[b] = received[...].astype(F32).T.astype(BF16)

    def origin_of(n):
        s = (n + 1) // 2
        away = jnp.where(n % 2 == 1, -s, s)
        for j, far in enumerate((-FAR, FAR, -FAR - 1, -FAR - 2, FAR + 1)):
            away = jnp.where(n == 2 * HOPS + 1 + j, far, away)
        return lax.rem(z + away + n_z, n_z)

    def ring_copy(m, origin, d, h):
        ref = table.at[origin * 2 + core, pl.ds(pl.multiple_of(h * PART, PART), PART), :]
        return pltpu.make_async_remote_copy(
            src_ref=ref, dst_ref=ref, send_sem=ring_send.at[m], recv_sem=ring_recv.at[m],
            device_id=(a, jnp.where(d == 0, up, down)), device_id_type=MESH)

    def half_copy(n, h, origin, who):
        ref = table.at[origin * 2 + who, half_rows(h), :]
        return pltpu.make_async_remote_copy(
            src_ref=ref, dst_ref=ref, send_sem=half_send.at[n * 2 + h], recv_sem=half_recv.at[n * 2 + h],
            device_id=(a, other), device_id_type=MESH)

    for h in range(PARTS):
        for d in range(2):
            ring_copy(h * 2 + d, z, d, h).start()
    for h in range(2):
        half_copy(0, h, z, core).start()

    def far_copy(g, to, frm):
        low, count = GROUPS[g]
        return pltpu.make_async_remote_copy(
            src_ref=far_picked.at[pl.ds(low, count), pl.ds(pl.multiple_of(to * cap, cap), cap), :],
            dst_ref=far_received.at[pl.ds(low, count), pl.ds(pl.multiple_of(frm * cap, cap), cap), :],
            send_sem=far_send.at[g * n_alpha + to], recv_sem=far_recv.at[g * n_alpha + frm],
            device_id=(to, b), device_id_type=MESH)

    def far_pick(g):
        low, count = GROUPS[g]
        for j in range(low, low + count):
            far_picked[j] = jnp.dot(hot[...], raw[j], preferred_element_type=F32).astype(BF16)

        @pl.loop(1, n_alpha)
        def _(o):
            far_copy(g, lax.rem(a + o, n_alpha), a).start()

        for j in range(low, low + count):
            far_received[j, mine, :] = far_picked[j, mine, :]

    def far_wait(g):
        @pl.loop(1, n_alpha)
        def _(o):
            far_copy(g, a, lax.rem(a + o, n_alpha)).wait_recv()

    def far_turn(j):
        n = 2 * HOPS + 1 + j
        origin = origin_of(n)
        table[origin * 2 + core] = far_received[j].astype(F32).T.astype(BF16)
        for h in range(2):
            half_copy(n, h, origin, core).start()

    def mix(k):
        n = jnp.where(k == 7, 11, jnp.where(k == 10, 12, jnp.where(k < 7, k, jnp.where(k < 10, k - 1, k - 2))))
        n = jnp.where(k > 10, jnp.where(k > 13, k - 5, k + 2), n)
        origin = origin_of(n)
        for h in range(2):
            half_copy(n, h, origin, 1 - core).wait_recv()
        rows = table[pl.ds(origin * 2, 2)].reshape(2 * BLK, slots)
        for p in range(0, NP, 2):
            r = jnp.dot(rows, w_t[:, p * BLK : (p + 2) * BLK], preferred_element_type=F32)
            for k in range(2):
                at = LEAD + (p + k) * 2 * cols + origin * (2 * BLK)
                x = r[:, k * BLK : (k + 1) * BLK]
                big[pl.ds(pl.multiple_of(at, 8), 2 * BLK), :] = x
                big[pl.ds(pl.multiple_of(at + cols, 8), 2 * BLK), :] = -x

    far_pick(0)
    w_wait().wait_recv()
    for p in range(NP):
        w_t[:, p * BLK : (p + 1) * BLK] = w_full[p].astype(F32).T.astype(BF16)

    def target(s):
        return jnp.maximum(jnp.maximum(2 * s - 1, 3 * s - 4), 0)

    @pl.loop(0, ROUND * HOPS)
    def _(m):
        s, d, h = m // ROUND + 1, m % 2, (m % ROUND) // 2
        origin = lax.rem(jnp.where(d == 0, z - s, z + s) + n_z, n_z)
        ring_copy(m, origin, d, h).wait_recv()

        @pl.when(s < HOPS)
        def _():
            ring_copy(m + ROUND, origin, d, h).start()

        @pl.when(h % 2 == 1)
        def _():
            half_copy(2 * s - 1 + d, h // 2, origin, core).start()

        @pl.when(m == ROUND - 1)
        def _():
            for j in range(2, 5):
                raw_copy(j).wait_recv()
            far_pick(1)

        low, high = target(s - 1), target(s)
        k = m % ROUND

        @pl.loop(low + ((high - low) * k) // ROUND, low + ((high - low) * (k + 1)) // ROUND)
        def _(n):
            mix(n)

        @pl.when(m == 3 * ROUND - 1)
        def _():
            far_wait(0)
            far_turn(0)

        @pl.when(m == 4 * ROUND - 1)
        def _():
            far_turn(1)

        @pl.when(m == 4 * ROUND + 2)
        def _():
            far_wait(1)

        for j in range(2, 5):
            @pl.when(m == 4 * ROUND + 1 + j)
            def _(j=j):
                far_turn(j)

    side = jnp.where(z % 2 == 1, 1, -1)
    mate = lax.rem(z - side + n_z, n_z)

    last = n_z - 1

    def place(i):
        own = jnp.logical_or(jnp.logical_and(i % 2 == 1, i >= 3), i == last - 1)
        t_own = jnp.where(i >= last - 1, i - steps, (i - 3) // 2)
        return own, jnp.where(own, t_own, jnp.where(i < 3, i, i // 2 + 1))

    def owner_of(i):
        own, t = place(i)
        far = steps - 1 - t
        return lax.rem(jnp.where(own, z + side * far, mate - side * far) + n_z, n_z)

    def idx_copy(i, which):
        chunk = owner_of(i) * 2 + jnp.where(which == 0, 1 - core, core)
        return pltpu.make_async_copy(idx_v.at[chunk], idx_s.at[which], idx_sem.at[which])

    for which in range(2):
        idx_copy(0, which).start()

    @pl.loop(3 * HOPS - 4, n_z)
    def _(n):
        mix(n)

    sub = lax.broadcasted_iota(I32, (8, BLK), 0)

    def gather(which, dst):
        for u in range(BLK // 8):
            total = None
            for k in range(8):
                acc = None
                for p in range(NP):
                    v = big[pl.ds(idx_s[which, p, u * 8 + k], 8), :]
                    acc = v if acc is None else acc + v
                total = acc if total is None else jnp.where(sub == k, acc, total)
            dst[u * 8 : (u + 1) * 8, :] = total

    def sib_copy(i):
        return pltpu.make_async_remote_copy(
            src_ref=sib_out.at[i], dst_ref=sib_in.at[i], send_sem=sib_send.at[i], recv_sem=sib_recv.at[i],
            device_id=(a, other), device_id_type=MESH)

    def mate_copy(t):
        return pltpu.make_async_remote_copy(
            src_ref=mate_out.at[t], dst_ref=mate_in.at[t], send_sem=mate_send.at[t], recv_sem=mate_recv.at[t],
            device_id=(a, mate * 2 + core), device_id_type=MESH)

    def rs_copy(t):
        return pltpu.make_async_remote_copy(
            src_ref=rs_out.at[t], dst_ref=rs_in.at[t], send_sem=rs_send.at[t], recv_sem=rs_recv.at[t],
            device_id=(a, lax.rem(z + side * (steps - 1 - t) + n_z, n_z) * 2 + core), device_id_type=MESH)

    def chip_sum(i):
        sib_copy(i).wait_recv()
        terms[i] = terms[i] + sib_in[i]

        own, t = place(i)

        @pl.when(jnp.logical_not(own))
        def _():
            mate_out[t] = terms[i].astype(BF16)
            mate_copy(t).start()

        @pl.when(jnp.logical_and(own, i < last))
        def _():
            mate_copy(t).wait_recv()
            rs_out[t] = (terms[i] + mate_in[t].astype(F32)).astype(BF16)
            rs_copy(t).start()

    @pl.loop(0, n_z)
    def _(i):
        idx_copy(i, 0).wait()
        gather(0, sib_out.at[i])
        sib_copy(i).start()

        @pl.when(i + 1 < n_z)
        def _():
            idx_copy(i + 1, 0).start()

        @pl.when(i > 0)
        def _():
            chip_sum(i - 1)

        idx_copy(i, 1).wait()
        gather(1, terms.at[i])

        @pl.when(i + 1 < n_z)
        def _():
            idx_copy(i + 1, 1).start()

    @pl.loop(1, n_alpha)
    def _(o):
        pick_copy(lax.rem(a + o, n_alpha), a).wait_send()

        for g in range(2):
            far_copy(g, lax.rem(a + o, n_alpha), a).wait_send()

    for j in range(5):
        raw_copy(j).wait_send()

    @pl.loop(0, ROUND * HOPS)
    def _(m):
        ring_copy(m, z, m % 2, (m % ROUND) // 2).wait_send()

    @pl.loop(0, 2 * n_z)
    def _(j):
        half_copy(j // 2, j % 2, z, core).wait_send()

    w_copy().wait_send()

    @pl.loop(0, n_z)
    def _(i):
        sib_copy(i).wait_send()

    @pl.loop(0, steps)
    def _(t):
        mate_copy(t).wait_send()

        @pl.when(t < steps - 1)
        def _():
            rs_copy(t).wait_send()

    chip_sum(last)
    mate_copy(steps - 1).wait_recv()
    total = terms[last] + mate_in[steps - 1].astype(F32)
    for t in range(steps - 1):
        rs_copy(t).wait_recv()
        total = total + rs_in[t].astype(F32)
    out[...] = total.T.astype(BF16)


def body(n_alpha, n_z, coeffs, send_rows, a_source, a_sign, b_source, b_sign, integrals):
    cap = send_rows.shape[1]
    slots = n_alpha * cap
    n_pairs = integrals.shape[0]
    cols = b_source.shape[1]
    V, DMA = pltpu.VMEM, pltpu.SemaphoreType.DMA
    blocks, half = 2 * n_z, n_z // 2
    scratch = [
        V((BLK, BLK), BF16), V(send_rows.shape, I32), V(a_source.shape, I32), V(a_sign.shape, I32),
        V(b_source.shape, I32), V(b_sign.shape, I32), V(integrals.shape, BF16),
        V((slots, BLK), BF16), V((slots, BLK), BF16), V((slots, BLK), BF16),
        V((5, BLK, BLK), BF16), V((5, slots, BLK), BF16), V((5, slots, BLK), BF16), V((blocks, BLK, slots), BF16),
        V((BLK, n_pairs), F32), V((BLK, n_pairs), F32), V((2 * NP, n_pairs), BF16),
        V((HALF, 2 * NP, slots), F32), V((NP, HALF, slots), BF16), V((NP, BLK, slots), BF16),
        V((slots, NP * BLK), BF16), V((NP * 2 * cols + 2 * LEAD, BLK), F32),
        V((cols // BLK, NP, BLK), I32), pltpu.SMEM((2, NP, BLK), I32),
        V((half, BLK, BLK), BF16), V((half, BLK, BLK), BF16), V((half, BLK, BLK), BF16), V((half, BLK, BLK), BF16),
        V((n_z, BLK, BLK), F32), V((n_z, BLK, BLK), F32), V((n_z, BLK, BLK), F32),
        DMA((n_alpha,)), DMA((n_alpha,)), DMA((5,)), DMA((5,)), DMA((2 * n_alpha,)), DMA((2 * n_alpha,)),
        DMA((ROUND * HOPS,)), DMA((ROUND * HOPS,)),
        DMA((2 * n_z,)), DMA((2 * n_z,)),
        DMA, DMA, DMA((half,)), DMA((half,)), DMA((half,)), DMA((half,)), DMA((n_z,)), DMA((n_z,)), DMA((2,)), DMA((7,)),
    ]
    return pl.pallas_call(
        functools.partial(kernel, n_alpha, n_z),
        out_shape=jax.ShapeDtypeStruct((BLK, BLK), BF16),
        in_specs=[pl.BlockSpec(memory_space=pl.ANY)] * 7,
        out_specs=pl.BlockSpec(memory_space=V),
        scratch_shapes=scratch,
        compiler_params=pltpu.CompilerParams(
            collective_id=0, has_side_effects=True, vmem_limit_bytes=60 * 2**20),
    )(coeffs, send_rows, a_source, a_sign, b_source, b_sign, integrals)


def solution(mesh):
    in_specs = (
        P("alpha", "beta"), P("alpha", None), P(None, "alpha"), P(None, "alpha"),
        P("beta", None), P("beta", None), P(),
    )
    run = functools.partial(body, mesh.shape["alpha"], mesh.shape["beta"] // 2)
    return jax.shard_map(run, mesh=mesh, in_specs=in_specs, out_specs=P("alpha", "beta"), check_vma=False)
```
